32 devices in a mesh: req: 16 (over z, x, core), tensor: 2 (over y).
Axes of the slice: x: 2, y: 2, z: 4, core: 2. Of those that a mesh axis runs over, the one named last changes fastest.
Arguments:
- tokens: bfloat16 [1024, 1024], P('req'), may hold values from -6 to 6
- norm_gain: float32 [1024], replicated, may hold values from 0.1 to 1.9
- w_qkv: bfloat16 [1024, 3, 1024], P(None, None, 'tensor'), may hold values from -0.1875 to 0.1875
- w_out: bfloat16 [1024, 1024], P('tensor'), may hold values from -0.25 to 0.25
- root_kv: bfloat16 [1024, 2, 1024], P('req', None, 'tensor'), may hold values from -60 to 60, as said below
- branch_kv: bfloat16 [16, 1024, 2, 1024], P('req', None, None, 'tensor'), may hold values from -60 to 60, as said below
- leaf_kv: bfloat16 [256, 16, 2, 1024], P('req', None, None, 'tensor'), may hold values from -60 to 60, as said below
- branch: int32 [256, 1], P('req'), may hold values from 0 to 15; in each aligned block of 16 rows (0 to 15, 16 to 31, ...) at most 2 rows name the same one
- node_owner: int32 [16], replicated, may hold values from 0 to 15, each once
- branch_len: int32 [16], replicated, may hold values from 1 to 1024, as said below
- leaf_len: int32 [256], P('req'), may hold values from 1 to 16
- new_count: int32 [256], P('req'), may hold values from 1 to 4
Outputs:
- attn_out: bfloat16 [1024, 1024], P('req', 'tensor')
The draws below stay inside these ranges and needn't reach their ends.
Inputs may be any that keep to these rules, and one draw needn't show every extreme that they name: Among the 16 requests of one device (aligned blocks of rows) no branch node is named more than 2 times; some node is named exactly 2 times. `node_owner`: each storage slot holds exactly one node. `branch_len`: some node has all 1024 positions. `root_kv`: Real-valued keys and values. `branch_kv`: Real-valued keys and values. `leaf_kv`: Real-valued keys and values.
All inputs are finite; a program needn't handle non-finite values.
Results may differ from the reference program's by a relative error of at most 0.0095.
The reference program's roundings to bfloat16 on the way count: a program that leaves them out, or rounds other values in their place, can miss the bound.
Values may be sent and summed in bfloat16 or wider, within the bound.
A program may use at most 64 MiB of HBM per device.

```python
import math
import jax
import jax.numpy as jnp
import numpy as np
from jax import lax

D = 1024
H = 16
HD = 64
NEWMAX = 4
REQ_DEV = 16
LEN1 = 1024
LEN2 = 16
REQUESTS = 256
ROWS = 1024
ROOT = 1024
NODES = 16
CAP = 2


def cache_draw(key, shape):
    key_one, key_two = jax.random.split(key, 2)
    half_shape = shape[:-2] + (1, shape[-1])
    key_part = jnp.clip(3.0 * jax.random.normal(key_one, half_shape, jnp.float32), -16.0, 16.0)
    value_part = jnp.clip(jax.random.normal(key_two, half_shape, jnp.float32), -6.0, 6.0)
    return jnp.concatenate([key_part, value_part], axis=-2).astype(jnp.bfloat16)


def draw_root_kv(key, part):
    return cache_draw(jax.random.fold_in(key, 11), (ROOT, 2, H * HD))


def draw_branch_kv(key, part):
    return cache_draw(jax.random.fold_in(key, 12), (NODES, LEN1, 2, H * HD))


def draw_leaf_kv(key, part):
    return cache_draw(jax.random.fold_in(key, 13), (REQUESTS, LEN2, 2, H * HD))


def draw_branch_len(key, part):
    key_one, key_two = jax.random.split(jax.random.fold_in(key, 14))
    lengths = jax.random.randint(key_one, (NODES,), 1, LEN1 + 1)
    longest = jax.random.randint(key_two, (), 0, NODES)
    return lengths.at[longest].set(LEN1).astype(jnp.int32)


def plant(entries, stream_key, least, high):
    spot = [jax.random.randint(jax.random.fold_in(stream_key, axis), (), 0, length) for axis, length in enumerate(entries.shape)]
    widest = entries.shape.index(max(entries.shape))
    beside = spot[:widest] + [(spot[widest] + 1) % entries.shape[widest]] + spot[widest + 1:]
    return entries.at[tuple(spot)].set(least).at[tuple(beside)].set(high)


def strengthened(values, rng, source, target, blocks, factor):
    owner, partner = [(jnp.arange(values.shape[position]) // (values.shape[position] // blocks)).reshape([-1 if axis == position else 1 for axis in range(values.ndim)]) for position in (source, target)]
    chosen = jax.random.permutation(rng, blocks)[partner]
    strong = (owner == chosen) | (owner == (partner + blocks // 2) % blocks)
    return jnp.where(strong, factor * values, values)


def level_of(stream_key, shape, pieces, least, high):
    factor_of = 1.0
    for dim, blocks in pieces:
        heights = jax.random.uniform(jax.random.fold_in(jax.random.fold_in(stream_key, 6), dim), (blocks,), jnp.float32, least / len(pieces), high / len(pieces))
        factor_of = factor_of * jnp.repeat(jnp.exp(heights), shape[dim] // blocks).reshape((-1,) + (1,) * (len(shape) - 1 - dim))
    return factor_of


def routed_block(own_key, own, number, rows, amount, top, most, lean):
    ranking = jax.random.permutation(own_key, amount)
    crowded, usual = portions_of(amount, rows * top, most, lean, True), portions_of(amount, rows * top, most, lean, False)
    places = jnp.arange(amount)

    def named(sizes, turn):
        used = int((sizes > 0).sum())
        fixed = max(1, used // 4)
        moved = fixed + (places - fixed + turn * (used - fixed)) % max(1, amount - fixed)
        return jnp.zeros((amount,), jnp.int32).at[ranking[jnp.where(places < fixed, places, moved)]].set(jnp.asarray(sizes, jnp.int32))

    sizes = jnp.where(number % 4 == 0, named(crowded, number // 4), named(usual, number - number // 4 - 1))
    mixed = jax.random.permutation(jax.random.fold_in(own, 3), amount)
    giver, sink = mixed[0:amount // 2 * 2:2], mixed[1:amount // 2 * 2:2]
    slack = jnp.minimum(sizes[giver] - 1, most - sizes[sink]) // 2
    slack = jnp.where((giver == ranking[0]) | (sink == ranking[0]) | (sizes[sink] == 0), 0, jnp.maximum(slack, 0))
    moved = jax.random.randint(jax.random.fold_in(own, 4), (amount // 2,), 0, 1 << 20) % (slack + 1)
    sizes = sizes.at[giver].add(-moved).at[sink].add(moved)
    labels = jnp.searchsorted(jnp.cumsum(sizes), jnp.arange(rows * top), side="right").astype(jnp.int32)
    listing = labels.reshape(top, rows).T
    listing = listing[jax.random.permutation(jax.random.fold_in(own, 1), rows)]
    turn = jax.random.randint(jax.random.fold_in(own, 2), (rows, 1), 0, top)
    return jnp.take_along_axis(listing, (jnp.arange(top)[None, :] + turn) % top, axis=1)


def portions_of(number_of, total, limit, lean, full):
    portions = [(1 << 20) // math.isqrt(grade ** lean) + 1 for grade in range(1, number_of + 1)]
    largest = limit if full else min(limit, max(-(-total // number_of), total * portions[0] // sum(portions)))
    least = 1 if total - largest >= number_of - 1 else 0
    counts, spare = [largest] + [least] * (number_of - 1), total - largest - least * (number_of - 1)
    while spare > 0:
        candidates = [i for i in range(1, number_of) if counts[i] < largest] or [i for i in range(1, number_of) if counts[i] < limit]
        mass, left = sum([portions[i] for i in candidates]), spare
        for i in candidates:
            more = min(limit - counts[i], max(1, left * portions[i] // mass), spare)
            counts[i] = counts[i] + more
            spare = spare - more
    return np.array(counts)


def bell_draw(stream_key, shape, scale, bound, shards=(), dtype=jnp.bfloat16):
    result = jax.random.normal(stream_key, shape, jnp.float32) * scale
    if len(shards) > 0:
        result = level_of(stream_key, shape, shards, -0.22, 0.18) * result
    return jnp.clip(result, min=-bound, max=bound).astype(dtype)


def heavy_noise(stream_key, shape, deviation, reach, shards, heavy, kind=jnp.bfloat16):
    array = deviation * jax.random.normal(stream_key, shape, jnp.float32)
    if shards:
        array = array * level_of(stream_key, shape, shards, -0.22, 0.18)
    return jnp.clip(strengthened(array, jax.random.fold_in(stream_key, 3), *heavy), -reach, reach).astype(kind)


def setup_inputs(seed: int = 0) -> dict:
    keys = jax.random.split(jax.random.key(seed), 13)
    tokens = bell_draw(keys[0], (ROWS, D), 1.0, 6.0, ((0, 16),))
    norm_gain = jnp.clip(1.0 + 0.18 * jax.random.normal(keys[1], (D,), jnp.float32), 0.1, 1.9)
    w_qkv = bell_draw(keys[2], (D, 3, H * HD), D ** -0.5, 0.1875, ((2, 2),))
    w_out = heavy_noise(keys[3], (H * HD, D), (H * HD) ** -0.5, 0.25, ((0, 2),), (0, 1, 2, 2.0))
    root_kv = draw_root_kv(jax.random.fold_in(keys[12], 71), 0)
    branch_kv = draw_branch_kv(jax.random.fold_in(keys[12], 71), 0)
    leaf_kv = draw_leaf_kv(jax.random.fold_in(keys[12], 71), 0)
    branch_keys = jax.random.split(jax.random.fold_in(keys[7], 1), REQUESTS // REQ_DEV)
    branch_turns = jax.random.permutation(jax.random.fold_in(keys[7], 3), REQUESTS // REQ_DEV)
    branch = jax.vmap(lambda own, number: routed_block(jax.random.fold_in(keys[7], 2), own, number, REQ_DEV, NODES, 1, CAP, 2))(branch_keys, branch_turns).reshape((REQUESTS, 1))
    node_owner = jax.random.permutation(keys[8], NODES).astype(jnp.int32)
    branch_len = draw_branch_len(jax.random.fold_in(keys[12], 71), 0)
    leaf_len = plant(jax.random.randint(keys[10], (REQUESTS,), 1, LEN2 + 1), jax.random.fold_in(keys[10], 1), 1, LEN2).astype(jnp.int32)
    new_count = plant(jax.random.randint(keys[11], (REQUESTS,), 1, NEWMAX + 1), jax.random.fold_in(keys[11], 1), 1, NEWMAX).astype(jnp.int32)
    return {"tokens": tokens, "norm_gain": norm_gain, "w_qkv": w_qkv, "w_out": w_out, "root_kv": root_kv, "branch_kv": branch_kv, "leaf_kv": leaf_kv, "branch": branch, "node_owner": node_owner, "branch_len": branch_len, "leaf_len": leaf_len, "new_count": new_count}


def partial_softmax(queries, key_rows, value_rows, usable):
    scores = jnp.einsum('qhe,khe->qhk', queries.astype(jnp.float32), key_rows.astype(jnp.float32)) * HD ** (-0.5)
    masked = jnp.where(usable[:, None, :], scores, -jnp.inf)
    peak = lax.optimization_barrier(jnp.max(masked, axis=2))
    weights = jnp.where(usable[:, None, :], jnp.exp(scores - peak[:, :, None]), 0.0)
    totals = lax.optimization_barrier(jnp.sum(weights, axis=2))
    rounded = weights.astype(jnp.bfloat16).astype(jnp.float32)
    weighted = jnp.einsum('qhk,khe->qhe', rounded, value_rows.astype(jnp.float32))
    return (peak, totals, weighted)

def reference(tokens, norm_gain, w_qkv, w_out, root_kv, branch_kv, leaf_kv, branch, node_owner, branch_len, leaf_len, new_count):
    floats = tokens.astype(jnp.float32)
    normed = (floats * lax.rsqrt(lax.optimization_barrier(jnp.mean(floats * floats, axis=1, keepdims=True)) + 1e-05) * norm_gain).astype(jnp.bfloat16)
    projected = jnp.dot(normed, w_qkv.reshape(D, 3 * H * HD), preferred_element_type=jnp.float32).astype(jnp.bfloat16)
    projected = projected.reshape(REQUESTS, NEWMAX, 3, H, HD)
    root_keys = root_kv[:, 0].reshape(ROOT, H, HD)
    root_values = root_kv[:, 1].reshape(ROOT, H, HD)
    owner_slot = node_owner[branch[:, 0]].astype(jnp.int32)
    stored_len = branch_len[branch[:, 0]]
    positions = jnp.arange(LEN2 + NEWMAX)
    shifted = positions - LEN2
    draft_pos = jnp.arange(NEWMAX)
    branch_pos = jnp.arange(LEN1)

    def serve(index):
        block = projected[index]
        queries = block[:, 0]
        root_state = partial_softmax(queries, root_keys, root_values, jnp.ones((NEWMAX, ROOT), jnp.bool_))
        cache = lax.dynamic_index_in_dim(branch_kv, owner_slot[index], 0, keepdims=False)
        usable = jnp.broadcast_to(branch_pos[None, :] < stored_len[index], (NEWMAX, LEN1))
        branch_state = partial_softmax(queries, cache[:, 0].reshape(LEN1, H, HD), cache[:, 1].reshape(LEN1, H, HD), usable)
        leaf = leaf_kv[index]
        local_keys = jnp.concatenate([leaf[:, 0].reshape(LEN2, H, HD), block[:, 1]], axis=0)
        local_values = jnp.concatenate([leaf[:, 1].reshape(LEN2, H, HD), block[:, 2]], axis=0)
        local_usable = jnp.where(positions[None, :] < LEN2, positions[None, :] < leaf_len[index], (shifted[None, :] <= draft_pos[:, None]) & (shifted[None, :] < new_count[index]))
        local_state = partial_softmax(queries, local_keys, local_values, local_usable)
        states = (root_state, branch_state, local_state)
        peak = jnp.maximum(jnp.maximum(root_state[0], branch_state[0]), local_state[0])
        totals = jnp.zeros((NEWMAX, H), jnp.float32)
        weighted = jnp.zeros((NEWMAX, H, HD), jnp.float32)
        for state in states:
            factor = jnp.exp(state[0] - peak)
            totals = totals + factor * state[1]
            weighted = weighted + factor[:, :, None] * state[2]
        return (weighted / totals[:, :, None]).reshape(NEWMAX, H * HD)

    def serve_bundle(indices):
        return jax.vmap(serve)(indices)
    bundles = jnp.arange(REQUESTS).astype(jnp.int32).reshape(-1, 16)
    attention = lax.map(serve_bundle, bundles).reshape(ROWS, H * HD).astype(jnp.bfloat16)
    product = jnp.dot(attention, w_out, preferred_element_type=jnp.float32)
    in_use = (jnp.arange(NEWMAX)[None, :] < new_count[:, None]).reshape(ROWS)
    return jnp.where(in_use[:, None], product, 0.0).astype(jnp.bfloat16)
```

```python
import functools
import math

import jax
import jax.numpy as jnp
from jax import lax
from jax.experimental import pallas as pl
from jax.experimental.pallas import tpu as pltpu
from jax.sharding import PartitionSpec as P

HD = 64
MESH = pl.DeviceIdType.MESH
F32 = jnp.float32
BF16 = jnp.bfloat16
SCALE = HD ** (-0.5) * math.log2(math.e)
LOG2E = math.log2(math.e)


def iota(shape, dim):
    return lax.broadcasted_iota(jnp.int32, shape, dim)


def dot(a, b):
    return jnp.dot(a, b, preferred_element_type=F32)


def dot_t(a, b):
    return lax.dot_general(a, b, (((1,), (1,)), ((), ())), preferred_element_type=F32)


def kernel(
    n, nt, drafts, cap,
    tok_ref, gain_ref, w_hbm, wout_hbm, root_ref, bkv_hbm, leaf_hbm,
    branch_ref, owner_ref, blen_ref, llen_ref, newc_ref,
    out_ref,
    w_ref, wout_ref, braw, lraw, kroot, vroot, kbr, vbr, kloc, vloc,
    oq, aq, bo, br, tb, tr, sbuf, pbuf, peak_buf, sum_buf, asked,
    local_sem, ring_send, ring_recv, sib_send, sib_recv,
    q_send, q_recv, b_send, b_recv, t_send, t_recv,
):
    rows = tok_ref.shape[0]
    requests = rows // drafts
    width = wout_hbm.shape[0]
    gw = min(width, 256)
    hg = gw // HD
    groups = width // gw
    cd = cap * drafts
    slot = oq.shape[1]
    span = bkv_hbm.shape[0]
    leaf_span = leaf_hbm.shape[0] // requests
    block = root_ref.shape[0]
    chips = n // 2
    half = chips // 2
    me = lax.axis_index("req")
    tn = lax.axis_index("tensor")

    loads = [pltpu.make_async_copy(w_hbm.at[j], w_ref.at[j], local_sem.at[j]) for j in range(3)]
    loads.append(pltpu.make_async_copy(bkv_hbm, braw, local_sem.at[3]))
    loads.append(pltpu.make_async_copy(leaf_hbm, lraw, local_sem.at[4]))
    loads.append(pltpu.make_async_copy(wout_hbm, wout_ref, local_sem.at[5]))
    for load in loads:
        load.start()

    barrier = pltpu.get_barrier_semaphore()

    def greet(j, carry):
        pl.semaphore_signal(
            barrier, inc=1, device_id=(lax.rem(me + j, n), tn), device_id_type=MESH
        )
        return carry

    lax.fori_loop(1, n, greet, 0)
    for j in range(1, nt):
        pl.semaphore_signal(
            barrier, inc=1, device_id=(me, lax.rem(tn + j, nt)), device_id_type=MESH
        )

    def split_rows(raw, count):
        pick = iota((2 * count, 2 * count), 0)
        col = iota((2 * count, 2 * count), 1)
        source = jnp.where(pick < count, 2 * pick, 2 * (pick - count) + 1)
        parted = dot((col == source).astype(BF16), raw).astype(BF16)
        return parted[:count], parted[count:]

    own_k, own_v = split_rows(root_ref.reshape(2 * block, width)[...], block)
    kroot[me] = own_k
    vroot[me] = own_v

    pl.semaphore_wait(barrier, n - 1 + nt - 1)

    core = lax.rem(me, 2)
    chip = lax.div(me, 2)
    zc = lax.div(chip, 2)
    xc = lax.rem(chip, 2)
    place = (1 - xc) * zc + xc * (2 * half - 1 - zc)

    def device_at(position):
        q = lax.rem(position + 2 * chips, chips)
        xq = lax.div(q, half)
        zq = (1 - xq) * q + xq * (2 * half - 1 - q)
        return (zq * 2 + xq) * 2 + core

    sibling = me + 1 - 2 * core
    stores = (kroot, vroot)

    def ring(direction, hop, j, outgoing):
        sign = 1 - 2 * direction
        origin = device_at(place - sign * (hop - 1 if outgoing else hop))
        return pltpu.make_async_remote_copy(
            src_ref=stores[j].at[origin], dst_ref=stores[j].at[origin],
            send_sem=ring_send.at[direction, hop, j], recv_sem=ring_recv.at[direction, hop, j],
            device_id=(device_at(place + sign), tn), device_id_type=MESH,
        )

    def share(index, offset, j, outgoing):
        origin = device_at(place + offset)
        if not outgoing:
            origin = origin + 1 - 2 * core
        return pltpu.make_async_remote_copy(
            src_ref=stores[j].at[origin], dst_ref=stores[j].at[origin],
            send_sem=sib_send.at[index, j], recv_sem=sib_recv.at[index, j],
            device_id=(sibling, tn), device_id_type=MESH,
        )

    def travels(direction, hop, j):
        return hop < half or (hop == half and j == direction)

    sent = []
    shared = []

    def send_on(direction, hop, j):
        if travels(direction, hop, j):
            copy = ring(direction, hop, j, True)
            copy.start()
            sent.append(copy)

    def send_share(index, offset, j):
        copy = share(index, offset, j, True)
        copy.start()
        sent.append(copy)
        shared.append((index, offset, j))

    def pump(hop):
        for j in range(2):
            for direction in range(2):
                if travels(direction, hop, j):
                    ring(direction, hop, j, False).wait_recv()
                    send_on(direction, hop + 1, j)
                    offset = -hop if direction == 0 else hop
                    send_share(direction * half + hop, offset, j)

    for j in range(2):
        for direction in range(2):
            send_on(direction, 1, j)
    for j in range(2):
        send_share(0, 0, j)

    floats = tok_ref[...].astype(F32)
    mean = jnp.mean(floats * floats, axis=1, keepdims=True)
    normed = (floats * lax.rsqrt(mean + 1e-05) * gain_ref[...]).astype(BF16)
    loads[0].wait()
    queries = dot(normed, w_ref[0]).astype(BF16)

    row_req = lax.div(iota((rows, requests), 0), drafts)
    at_req = row_req == iota((rows, requests), 1)

    def per_row(values):
        return jnp.sum(jnp.where(at_req, values.astype(F32), 0.0), axis=1, keepdims=True)

    node_of = per_row(branch_ref[...])
    chosen = (node_of == iota((rows, n), 1).astype(F32)).astype(BF16)
    owners = (owner_ref[...] == iota((n, n), 0)).astype(BF16)
    target = dot_t(chosen, owners).astype(BF16)
    target_t = dot_t(owners, chosen).astype(BF16)
    same = dot_t(target, target)
    ri, rj = iota((rows, rows), 0), iota((rows, rows), 1)
    qi, qj = lax.div(ri, drafts), lax.div(rj, drafts)
    first_j = lax.rem(rj, drafts) == 0
    first_i = lax.rem(ri, drafts) == 0
    order_col = jnp.sum(jnp.where((qj < qi) & first_j, same, 0.0), axis=1, keepdims=True)
    order_row = jnp.sum(jnp.where((qi < qj) & first_i, same, 0.0), axis=0, keepdims=True)
    total = n * slot
    spread = (lax.div(iota((total, n), 0), slot) == iota((total, n), 1)).astype(BF16)

    def slot_parts(shape, dim):
        inner = lax.rem(iota(shape, dim), slot)
        item = lax.rem(inner, cd)
        return lax.div(inner, cd), lax.div(item, drafts).astype(F32), lax.rem(item, drafts)

    group_k, item_k, draft_k = slot_parts((total, rows), 0)
    put = (dot(spread, target_t) > 0.5) & (order_row == item_k) & (
        lax.rem(iota((total, rows), 1), drafts) == draft_k
    )
    packed = jnp.zeros((total, gw), F32)
    for g in range(groups):
        mine = jnp.where(put & (group_k == g), 1.0, 0.0).astype(BF16)
        packed = packed + dot(mine, queries[:, g * gw : (g + 1) * gw])
    oq[...] = packed.astype(BF16).reshape(n, slot, gw)
    aq[me] = oq[me]

    def exchange(source, landing, send_sem, recv_sem, j, outgoing):
        there = lax.rem(me + j, n)
        here = me if outgoing else lax.rem(me + n - j, n)
        return pltpu.make_async_remote_copy(
            src_ref=source.at[there], dst_ref=landing.at[here],
            send_sem=send_sem.at[j], recv_sem=recv_sem.at[j],
            device_id=(there, tn), device_id_type=MESH,
        )

    for j in range(1, n):
        exchange(oq, aq, q_send, q_recv, j, True).start()

    pump(1)

    loads[1].wait()
    own_keys = dot(normed, w_ref[1]).astype(BF16)
    loads[2].wait()
    own_values = dot(normed, w_ref[2]).astype(BF16)

    loads[3].wait()
    piece = min(128, span)
    braw_rows = braw.reshape(2 * span, width)

    def part_branch(b, carry):
        raw = braw_rows[pl.ds(pl.multiple_of(2 * piece * b, 2 * piece), 2 * piece), :]
        k_part, v_part = split_rows(raw, piece)
        at = pl.ds(pl.multiple_of(piece * b, piece), piece)
        kbr[at, :] = k_part
        vbr[at, :] = v_part
        return carry

    lax.fori_loop(0, span // piece, part_branch, 0)

    if half >= 2:
        pump(2)

    col_head = lax.div(iota((1, gw), 1), HD)

    def stack(part):
        return jnp.concatenate(
            [jnp.where(col_head == h, part, 0.0) for h in range(hg)], axis=0
        ).astype(BF16)

    def attend(scores, mask, values):
        peaks, sums, weights = [], [], []
        for s, keep in zip(scores, mask):
            if keep is not None:
                s = jnp.where(keep, s, -1e30)
            peak = jnp.max(s, axis=1, keepdims=True)
            w = jnp.exp2((s - peak) * SCALE)
            peaks.append(peak)
            sums.append(jnp.sum(w, axis=1, keepdims=True))
            weights.append(w.astype(BF16))
        weighted = dot(jnp.concatenate(weights, axis=0), values)
        return peaks, sums, weighted

    def attend_long(stacked_rows, keys_of, values_of, keep, step):
        amount_of, length = stacked_rows.shape[0], keys_of.shape[0]
        sbuf[:amount_of, :length] = dot_t(stacked_rows, keys_of)

        def some(c, carry):
            at = pl.ds(pl.multiple_of(c * step, step), step)
            s = sbuf[at, :length]
            if keep is not None:
                s = jnp.where(keep, s, -1e30)
            peak = jnp.max(s, axis=1, keepdims=True)
            w = jnp.exp2((s - peak) * SCALE)
            peak_buf[at, :] = jnp.broadcast_to(peak, (step, 128))
            sum_buf[at, :] = jnp.broadcast_to(jnp.sum(w, axis=1, keepdims=True), (step, 128))
            pbuf[at, :length] = w.astype(BF16)
            return carry

        lax.fori_loop(0, amount_of // step, some, 0)
        weighted = dot(pbuf[:amount_of, :length], values_of)
        return peak_buf[:amount_of, :1], sum_buf[:amount_of, :1], weighted

    for j in range(1, n):
        exchange(oq, aq, q_send, q_recv, j, False).wait_recv()
    asked[...] = aq[...].astype(F32)
    owned = jnp.sum(
        jnp.where(owner_ref[...] == me, blen_ref[...], 0).astype(F32), axis=1, keepdims=True
    )
    usable = iota((1, span), 1).astype(F32) < owned
    count = n * cd
    lane = iota((1, 128), 1)
    slabs = []
    for g in range(groups):
        part = asked[:, g * cd : (g + 1) * cd, :].reshape(count, gw)
        cols = slice(g * gw, (g + 1) * gw)
        peaks, sums, weighted = attend_long(stack(part), kbr[:, cols], vbr[:, cols], usable, 128)
        inverse = 1.0 / sums
        level = peaks * SCALE + jnp.log(sums) * LOG2E
        mixed = jnp.zeros((count, gw), F32)
        levels = jnp.zeros((count, 128), F32)
        for h in range(hg):
            at = slice(h * count, (h + 1) * count)
            mixed = jnp.where(col_head == h, weighted[at] * inverse[at], mixed)
            levels = jnp.where(lax.rem(lane, hg) == h, level[at], levels)
        high = levels.astype(BF16).astype(F32)
        middle = (levels - high).astype(BF16).astype(F32)
        low = levels - high - middle
        stats = jnp.where(lane < hg, high, jnp.where(lane < 2 * hg, middle, low))
        stats = jnp.where(lane < 3 * hg, stats, 0.0)
        slabs.append(jnp.concatenate([mixed, stats], axis=1).reshape(n, cd, gw + 128))
        if half >= 3 and g == 0:
            pump(3)
    if groups * cd < slot:
        slabs.append(jnp.zeros((n, slot - groups * cd, gw + 128), F32))
    bo[...] = jnp.concatenate(slabs, axis=1).astype(BF16)
    br[me] = bo[me]
    for j in range(1, n):
        exchange(bo, br, b_send, b_recv, j, True).start()

    loads[4].wait()
    leaf_rows = requests * leaf_span
    lpiece = min(128, leaf_rows)
    lraw_rows = lraw.reshape(2 * leaf_rows, width)

    def part_leaf(b, carry):
        raw = lraw_rows[pl.ds(pl.multiple_of(2 * lpiece * b, 2 * lpiece), 2 * lpiece), :]
        k_part, v_part = split_rows(raw, lpiece)
        at = pl.ds(pl.multiple_of(lpiece * b, lpiece), lpiece)
        kloc[at, :] = k_part
        vloc[at, :] = v_part
        return carry

    lax.fori_loop(0, leaf_rows // lpiece, part_leaf, 0)
    kloc[pl.ds(leaf_rows, rows), :] = own_keys
    vloc[pl.ds(leaf_rows, rows), :] = own_values
    keys = leaf_rows + rows
    leaf_len = per_row(llen_ref[...])
    new_count = per_row(newc_ref[...])
    ki, kj = iota((rows, keys), 0), iota((rows, keys), 1)
    own_j = kj - leaf_rows
    draft_j = lax.rem(jnp.maximum(own_j, 0), drafts)
    in_leaf = (
        (lax.div(kj, leaf_span) == lax.div(ki, drafts))
        & (lax.rem(kj, leaf_span).astype(F32) < leaf_len)
    )
    in_own = (
        (lax.div(jnp.maximum(own_j, 0), drafts) == lax.div(ki, drafts))
        & (draft_j <= lax.rem(ki, drafts))
        & (draft_j.astype(F32) < new_count)
    )
    local_keep = ((kj < leaf_rows) & in_leaf) | ((kj >= leaf_rows) & in_own)
    stacked = [stack(queries[:, g * gw : (g + 1) * gw].astype(F32)) for g in range(groups)]
    local_states = []
    for g in range(groups):
        cols = slice(g * gw, (g + 1) * gw)
        scores = dot_t(stacked[g], kloc[:, cols])
        pieces = [scores[h * rows : (h + 1) * rows] for h in range(hg)]
        local_states.append(attend(pieces, [local_keep] * hg, vloc[:, cols]))

    for hop in range(1 if half < 2 else 4 if half >= 3 else 3, half + 1):
        if hop > 1:
            pump(hop)
    for index, offset, j in shared:
        share(index, offset, j, False).wait_recv()

    before = []
    for g in range(groups):
        cols = slice(g * gw, (g + 1) * gw)
        root_keys = kroot[:, :, cols].reshape(n * block, gw)
        root_values = vroot[:, :, cols].reshape(n * block, gw)
        peaks, sums, weighted = attend_long(stacked[g], root_keys, root_values, None, rows)
        lpeaks, lsums, lweighted = local_states[g]
        level = jnp.zeros((rows, gw), F32)
        amount = jnp.zeros((rows, gw), F32)
        mixed = jnp.zeros((rows, gw), F32)
        for h in range(hg):
            at = slice(h * rows, (h + 1) * rows)
            top = jnp.maximum(peaks[at], lpeaks[h])
            one = jnp.exp2((peaks[at] - top) * SCALE)
            two = jnp.exp2((lpeaks[h] - top) * SCALE)
            level = jnp.where(col_head == h, top * SCALE, level)
            amount = jnp.where(col_head == h, one * sums[at] + two * lsums[h], amount)
            mixed = jnp.where(col_head == h, one * weighted[at] + two * lweighted[at], mixed)
        before.append((level, amount, mixed))

    group_l, item_l, draft_l = slot_parts((rows, total), 1)
    take = (dot_t(target, spread) > 0.5) & (order_col == item_l) & (
        lax.rem(iota((rows, total), 0), drafts) == draft_l
    )
    takes = [jnp.where(take & (group_l == g), 1.0, 0.0).astype(BF16) for g in range(groups)]
    loads[5].wait()

    for j in range(1, n):
        exchange(bo, br, b_send, b_recv, j, False).wait_recv()
    flat = br[...].reshape(total, gw + 128)
    heads = []
    for g in range(groups):
        got = dot(takes[g], flat)
        stats = got[:, gw:]
        level, amount, mixed = before[g]
        other = jnp.zeros((rows, gw), F32)
        for h in range(hg):
            joined = (
                stats[:, h : h + 1]
                + stats[:, hg + h : hg + h + 1]
                + stats[:, 2 * hg + h : 2 * hg + h + 1]
            )
            other = jnp.where(col_head == h, joined, other)
        top = jnp.maximum(level, other)
        one = jnp.exp2(level - top)
        two = jnp.exp2(other - top)
        heads.append(((one * mixed + two * got[:, :gw]) / (one * amount + two)).astype(BF16))
    attention = heads[0] if groups == 1 else jnp.concatenate(heads, axis=1)
    ow = out_ref.shape[1]
    for t in range(nt):
        tb[t] = dot(attention, wout_ref[:, t * ow : (t + 1) * ow])

    def reduce_copy(j, outgoing):
        there = lax.rem(tn + j, nt)
        here = tn if outgoing else lax.rem(tn + nt - j, nt)
        return pltpu.make_async_remote_copy(
            src_ref=tb.at[there], dst_ref=tr.at[here],
            send_sem=t_send.at[j], recv_sem=t_recv.at[j],
            device_id=(me, there), device_id_type=MESH,
        )

    for j in range(1, nt):
        reduce_copy(j, True).start()
    in_use = lax.rem(iota((rows, 1), 0), drafts).astype(F32) < new_count
    result = tb[tn]
    for copy in sent:
        copy.wait_send()
    for j in range(1, n):
        exchange(oq, aq, q_send, q_recv, j, True).wait_send()
        exchange(bo, br, b_send, b_recv, j, True).wait_send()
    for j in range(1, nt):
        reduce_copy(j, False).wait_recv()
        result = result + tr[lax.rem(tn + nt - j, nt)]
    out_ref[...] = jnp.where(in_use, result, 0.0).astype(BF16)
    for j in range(1, nt):
        reduce_copy(j, True).wait_send()


def local(
    n, nt,
    tokens, norm_gain, w_qkv, w_out, root_kv, branch_kv, leaf_kv,
    branch, node_owner, branch_len, leaf_len, new_count,
):
    rows, depth = tokens.shape
    requests = branch.shape[0]
    drafts = rows // requests
    nodes = node_owner.shape[0]
    width = w_out.shape[0]
    ow = w_out.shape[1] // nt
    cap = max(2, 2 * requests // nodes)
    gw = min(width, 256)
    slot = max(16, width // gw * cap * drafts)
    block = root_kv.shape[0]
    span = branch_kv.shape[1]
    leaf_rows = leaf_kv.shape[0] * leaf_kv.shape[1]
    half = n // 4
    long_rows = gw // HD * max(n * cap * drafts, rows)
    longest = max(span, n * block)
    vmem = pl.BlockSpec(memory_space=pltpu.VMEM)
    hbm = pl.BlockSpec(memory_space=pl.ANY)
    dma = pltpu.SemaphoreType.DMA
    return pl.pallas_call(
        functools.partial(kernel, n, nt, drafts, cap),
        out_shape=jax.ShapeDtypeStruct((rows, ow), BF16),
        in_specs=[vmem, vmem, hbm, hbm, vmem, hbm, hbm] + [vmem] * 5,
        out_specs=vmem,
        scratch_shapes=[
            pltpu.VMEM((3, depth, width), BF16),
            pltpu.VMEM(w_out.shape, BF16),
            pltpu.VMEM((span, 2, width), BF16),
            pltpu.VMEM((leaf_rows, 2, width), BF16),
            pltpu.VMEM((n, block, width), BF16),
            pltpu.VMEM((n, block, width), BF16),
            pltpu.VMEM((span, width), BF16),
            pltpu.VMEM((span, width), BF16),
            pltpu.VMEM((leaf_rows + rows, width), BF16),
            pltpu.VMEM((leaf_rows + rows, width), BF16),
            pltpu.VMEM((n, slot, gw), BF16),
            pltpu.VMEM((n, slot, gw), BF16),
            pltpu.VMEM((n, slot, gw + 128), BF16),
            pltpu.VMEM((n, slot, gw + 128), BF16),
            pltpu.VMEM((nt, rows, ow), F32),
            pltpu.VMEM((nt, rows, ow), F32),
            pltpu.VMEM((long_rows, longest), F32),
            pltpu.VMEM((long_rows, longest), BF16),
            pltpu.VMEM((long_rows, 128), F32),
            pltpu.VMEM((long_rows, 128), F32),
            pltpu.VMEM((n, slot, gw), F32),
            dma((6,)),
            dma((2, half + 1, 2)),
            dma((2, half + 1, 2)),
            dma((2 * half + 1, 2)),
            dma((2 * half + 1, 2)),
            dma((n,)),
            dma((n,)),
            dma((n,)),
            dma((n,)),
            dma((nt,)),
            dma((nt,)),
        ],
        compiler_params=pltpu.CompilerParams(
            collective_id=0, has_side_effects=True, vmem_limit_bytes=58 << 20
        ),
    )(
        tokens,
        norm_gain.reshape(1, -1),
        jnp.transpose(w_qkv, (1, 0, 2)),
        w_out,
        root_kv,
        branch_kv.reshape(span, 2, width),
        leaf_kv.reshape(leaf_rows, 2, width),
        branch.reshape(1, requests),
        node_owner.reshape(1, nodes),
        branch_len.reshape(1, nodes),
        leaf_len.reshape(1, requests),
        new_count.reshape(1, requests),
    )


def solution(mesh):
    placed = (
        P("req", None),
        P(),
        P(None, None, "tensor"),
        P("tensor", None),
        P("req", None, "tensor"),
        P("req", None, None, "tensor"),
        P("req", None, None, "tensor"),
        P("req", None),
        P(),
        P(),
        P("req"),
        P("req"),
    )
    return jax.shard_map(
        functools.partial(local, mesh.shape["req"], mesh.shape["tensor"]),
        mesh=mesh, in_specs=placed, out_specs=P("req", "tensor"), check_vma=False,
    )
```

```python
import functools
import math

import jax
import jax.numpy as jnp
from jax import lax
from jax.experimental import pallas as pl
from jax.experimental.pallas import tpu as pltpu
from jax.sharding import PartitionSpec as P

HD = 64
MESH = pl.DeviceIdType.MESH
F32 = jnp.float32
BF16 = jnp.bfloat16
SCALE = HD ** (-0.5) * math.log2(math.e)
LOG2E = math.log2(math.e)


def iota(shape, dim):
    return lax.broadcasted_iota(jnp.int32, shape, dim)


def dot(a, b):
    return jnp.dot(a, b, preferred_element_type=F32)


def dot_t(a, b):
    return lax.dot_general(a, b, (((1,), (1,)), ((), ())), preferred_element_type=F32)


def kernel(
    n, nt, drafts, cap,
    tok_ref, gain_ref, w_hbm, wout_hbm, root_ref, bkv_hbm, leaf_hbm,
    branch_ref, owner_ref, blen_ref, llen_ref, newc_ref,
    out_ref,
    w_ref, wout_ref, braw, lraw, kroot, vroot, kbr, vbr, kloc, vloc,
    oq, aq, bo, br, tb, tr, sbuf, pbuf, peak_buf, sum_buf, asked,
    local_sem, ring_send, ring_recv, sib_send, sib_recv,
    q_send, q_recv, b_send, b_recv, t_send, t_recv,
):
    rows = tok_ref.shape[0]
    requests = rows // drafts
    width = wout_hbm.shape[0]
    gw = min(width, 256)
    hg = gw // HD
    groups = width // gw
    cd = cap * drafts
    slot = oq.shape[1]
    span = bkv_hbm.shape[0]
    leaf_span = leaf_hbm.shape[0] // requests
    block = root_ref.shape[0]
    chips = n // 2
    half = chips // 2
    me = lax.axis_index("req")
    tn = lax.axis_index("tensor")

    loads = [pltpu.make_async_copy(w_hbm.at[j], w_ref.at[j], local_sem.at[j]) for j in range(3)]
    loads.append(pltpu.make_async_copy(bkv_hbm, braw, local_sem.at[3]))
    loads.append(pltpu.make_async_copy(leaf_hbm, lraw, local_sem.at[4]))
    loads.append(pltpu.make_async_copy(wout_hbm, wout_ref, local_sem.at[5]))
    for load in loads:
        load.start()

    barrier = pltpu.get_barrier_semaphore()

    def greet(j, carry):
        pl.semaphore_signal(
            barrier, inc=1, device_id=(lax.rem(me + j, n), tn), device_id_type=MESH
        )
        return carry

    lax.fori_loop(1, n, greet, 0)
    for j in range(1, nt):
        pl.semaphore_signal(
            barrier, inc=1, device_id=(me, lax.rem(tn + j, nt)), device_id_type=MESH
        )

    def split_rows(raw, count):
        pick = iota((2 * count, 2 * count), 0)
        col = iota((2 * count, 2 * count), 1)
        source = jnp.where(pick < count, 2 * pick, 2 * (pick - count) + 1)
        parted = dot((col == source).astype(BF16), raw).astype(BF16)
        return parted[:count], parted[count:]

    own_k, own_v = split_rows(root_ref.reshape(2 * block, width)[...], block)
    kroot[me] = own_k
    vroot[me] = own_v

    core = lax.rem(me, 2)
    chip = lax.div(me, 2)
    zc = lax.div(chip, 2)
    xc = lax.rem(chip, 2)
    place = (1 - xc) * zc + xc * (2 * half - 1 - zc)

    def device_at(position):
        q = lax.rem(position + 2 * chips, chips)
        xq = lax.div(q, half)
        zq = (1 - xq) * q + xq * (2 * half - 1 - q)
        return (zq * 2 + xq) * 2 + core

    sibling = me + 1 - 2 * core
    stores = (kroot, vroot)

    def ring(direction, hop, j, outgoing):
        sign = 1 - 2 * direction
        origin = device_at(place - sign * (hop - 1 if outgoing else hop))
        return pltpu.make_async_remote_copy(
            src_ref=stores[j].at[origin], dst_ref=stores[j].at[origin],
            send_sem=ring_send.at[direction, hop, j], recv_sem=ring_recv.at[direction, hop, j],
            device_id=(device_at(place + sign), tn), device_id_type=MESH,
        )

    def share(index, offset, j, outgoing):
        origin = device_at(place + offset)
        if not outgoing:
            origin = origin + 1 - 2 * core
        return pltpu.make_async_remote_copy(
            src_ref=stores[j].at[origin], dst_ref=stores[j].at[origin],
            send_sem=sib_send.at[index, j], recv_sem=sib_recv.at[index, j],
            device_id=(sibling, tn), device_id_type=MESH,
        )

    def travels(direction, hop, j):
        return hop < half or (hop == half and j == direction)

    sent = []
    shared = []

    def send_on(direction, hop, j):
        if travels(direction, hop, j):
            copy = ring(direction, hop, j, True)
            copy.start()
            sent.append(copy)

    def send_share(index, offset, j):
        copy = share(index, offset, j, True)
        copy.start()
        sent.append(copy)
        shared.append((index, offset, j))

    def pump(hop):
        for j in range(2):
            for direction in range(2):
                if travels(direction, hop, j):
                    ring(direction, hop, j, False).wait_recv()
                    send_on(direction, hop + 1, j)
                    offset = -hop if direction == 0 else hop
                    send_share(direction * half + hop, offset, j)

    floats = tok_ref[...].astype(F32)
    mean = jnp.mean(floats * floats, axis=1, keepdims=True)
    normed = (floats * lax.rsqrt(mean + 1e-05) * gain_ref[...]).astype(BF16)
    loads[0].wait()
    queries = dot(normed, w_ref[0]).astype(BF16)

    row_req = lax.div(iota((rows, requests), 0), drafts)
    at_req = row_req == iota((rows, requests), 1)

    def per_row(values):
        return jnp.sum(jnp.where(at_req, values.astype(F32), 0.0), axis=1, keepdims=True)

    node_of = per_row(branch_ref[...])
    chosen = (node_of == iota((rows, n), 1).astype(F32)).astype(BF16)
    owners = (owner_ref[...] == iota((n, n), 0)).astype(BF16)
    target = dot_t(chosen, owners).astype(BF16)
    target_t = dot_t(owners, chosen).astype(BF16)
    same = dot_t(target, target)
    ri, rj = iota((rows, rows), 0), iota((rows, rows), 1)
    qi, qj = lax.div(ri, drafts), lax.div(rj, drafts)
    first_j = lax.rem(rj, drafts) == 0
    first_i = lax.rem(ri, drafts) == 0
    order_col = jnp.sum(jnp.where((qj < qi) & first_j, same, 0.0), axis=1, keepdims=True)
    order_row = jnp.sum(jnp.where((qi < qj) & first_i, same, 0.0), axis=0, keepdims=True)
    total = n * slot
    spread = (lax.div(iota((total, n), 0), slot) == iota((total, n), 1)).astype(BF16)

    def slot_parts(shape, dim):
        inner = lax.rem(iota(shape, dim), slot)
        item = lax.rem(inner, cd)
        return lax.div(inner, cd), lax.div(item, drafts).astype(F32), lax.rem(item, drafts)

    group_k, item_k, draft_k = slot_parts((total, rows), 0)
    put = (dot(spread, target_t) > 0.5) & (order_row == item_k) & (
        lax.rem(iota((total, rows), 1), drafts) == draft_k
    )
    packed = jnp.zeros((total, gw), F32)
    for g in range(groups):
        mine = jnp.where(put & (group_k == g), 1.0, 0.0).astype(BF16)
        packed = packed + dot(mine, queries[:, g * gw : (g + 1) * gw])
    oq[...] = packed.astype(BF16).reshape(n, slot, gw)
    aq[me] = oq[me]

    def exchange(source, landing, send_sem, recv_sem, j, outgoing):
        there = lax.rem(me + j, n)
        here = me if outgoing else lax.rem(me + n - j, n)
        return pltpu.make_async_remote_copy(
            src_ref=source.at[there], dst_ref=landing.at[here],
            send_sem=send_sem.at[j], recv_sem=recv_sem.at[j],
            device_id=(there, tn), device_id_type=MESH,
        )

    pl.semaphore_wait(barrier, n - 1 + nt - 1)
    for j in range(1, n):
        exchange(oq, aq, q_send, q_recv, j, True).start()
    for j in range(2):
        for direction in range(2):
            send_on(direction, 1, j)
    for j in range(2):
        send_share(0, 0, j)

    loads[1].wait()
    own_keys = dot(normed, w_ref[1]).astype(BF16)
    loads[2].wait()
    own_values = dot(normed, w_ref[2]).astype(BF16)

    loads[3].wait()
    piece = min(128, span)
    braw_rows = braw.reshape(2 * span, width)

    def part_branch(b, carry):
        raw = braw_rows[pl.ds(pl.multiple_of(2 * piece * b, 2 * piece), 2 * piece), :]
        k_part, v_part = split_rows(raw, piece)
        at = pl.ds(pl.multiple_of(piece * b, piece), piece)
        kbr[at, :] = k_part
        vbr[at, :] = v_part
        return carry

    lax.fori_loop(0, span // piece, part_branch, 0)

    col_head = lax.div(iota((1, gw), 1), HD)

    def stack(part):
        return jnp.concatenate(
            [jnp.where(col_head == h, part, 0.0) for h in range(hg)], axis=0
        ).astype(BF16)

    def attend(scores, mask, values):
        peaks, sums, weights = [], [], []
        for s, keep in zip(scores, mask):
            if keep is not None:
                s = jnp.where(keep, s, -1e30)
            peak = jnp.max(s, axis=1, keepdims=True)
            w = jnp.exp2((s - peak) * SCALE)
            peaks.append(peak)
            sums.append(jnp.sum(w, axis=1, keepdims=True))
            weights.append(w.astype(BF16))
        weighted = dot(jnp.concatenate(weights, axis=0), values)
        return peaks, sums, weighted

    def attend_long(stacked_rows, keys_of, values_of, keep, step):
        amount_of, length = stacked_rows.shape[0], keys_of.shape[0]
        sbuf[:amount_of, :length] = dot_t(stacked_rows, keys_of)

        def some(c, carry):
            for part in range(0, step, 32):
                at = pl.ds(pl.multiple_of(c * step + part, 32), 32)
                s = sbuf[at, :length]
                if keep is not None:
                    s = jnp.where(keep, s, -1e30)
                peak = jnp.max(s, axis=1, keepdims=True)
                w = jnp.exp2((s - peak) * SCALE)
                peak_buf[at, :] = jnp.broadcast_to(peak, (32, 128))
                sum_buf[at, :] = jnp.broadcast_to(jnp.sum(w, axis=1, keepdims=True), (32, 128))
                pbuf[at, :length] = w.astype(BF16)
            return carry

        lax.fori_loop(0, amount_of // step, some, 0)
        weighted = dot(pbuf[:amount_of, :length], values_of)
        return peak_buf[:amount_of, :1], sum_buf[:amount_of, :1], weighted

    loads[4].wait()
    leaf_rows = requests * leaf_span
    lpiece = min(128, leaf_rows)
    lraw_rows = lraw.reshape(2 * leaf_rows, width)

    def part_leaf(b, carry):
        raw = lraw_rows[pl.ds(pl.multiple_of(2 * lpiece * b, 2 * lpiece), 2 * lpiece), :]
        k_part, v_part = split_rows(raw, lpiece)
        at = pl.ds(pl.multiple_of(lpiece * b, lpiece), lpiece)
        kloc[at, :] = k_part
        vloc[at, :] = v_part
        return carry

    lax.fori_loop(0, leaf_rows // lpiece, part_leaf, 0)
    kloc[pl.ds(leaf_rows, rows), :] = own_keys
    vloc[pl.ds(leaf_rows, rows), :] = own_values
    keys = leaf_rows + rows
    leaf_len = per_row(llen_ref[...])
    new_count = per_row(newc_ref[...])
    ki, kj = iota((rows, keys), 0), iota((rows, keys), 1)
    own_j = kj - leaf_rows
    draft_j = lax.rem(jnp.maximum(own_j, 0), drafts)
    in_leaf = (
        (lax.div(kj, leaf_span) == lax.div(ki, drafts))
        & (lax.rem(kj, leaf_span).astype(F32) < leaf_len)
    )
    in_own = (
        (lax.div(jnp.maximum(own_j, 0), drafts) == lax.div(ki, drafts))
        & (draft_j <= lax.rem(ki, drafts))
        & (draft_j.astype(F32) < new_count)
    )
    local_keep = ((kj < leaf_rows) & in_leaf) | ((kj >= leaf_rows) & in_own)
    stacked = [stack(queries[:, g * gw : (g + 1) * gw].astype(F32)) for g in range(groups)]
    local_states = []
    for g in range(groups):
        cols = slice(g * gw, (g + 1) * gw)
        scores = dot_t(stacked[g], kloc[:, cols])
        pieces = [scores[h * rows : (h + 1) * rows] for h in range(hg)]
        local_states.append(attend(pieces, [local_keep] * hg, vloc[:, cols]))

    pump(1)

    for j in range(1, n):
        exchange(oq, aq, q_send, q_recv, j, False).wait_recv()
    asked[...] = aq[...].astype(F32)
    owned = jnp.sum(
        jnp.where(owner_ref[...] == me, blen_ref[...], 0).astype(F32), axis=1, keepdims=True
    )
    usable = iota((1, span), 1).astype(F32) < owned
    count = n * cd
    lane = iota((1, 128), 1)
    slabs = []
    for g in range(groups):
        part = asked[:, g * cd : (g + 1) * cd, :].reshape(count, gw)
        cols = slice(g * gw, (g + 1) * gw)
        peaks, sums, weighted = attend_long(stack(part), kbr[:, cols], vbr[:, cols], usable, 128)
        inverse = 1.0 / sums
        level = peaks * SCALE + jnp.log(sums) * LOG2E
        mixed = jnp.zeros((count, gw), F32)
        levels = jnp.zeros((count, 128), F32)
        for h in range(hg):
            at = slice(h * count, (h + 1) * count)
            mixed = jnp.where(col_head == h, weighted[at] * inverse[at], mixed)
            levels = jnp.where(lax.rem(lane, hg) == h, level[at], levels)
        high = levels.astype(BF16).astype(F32)
        middle = (levels - high).astype(BF16).astype(F32)
        low = levels - high - middle
        stats = jnp.where(lane < hg, high, jnp.where(lane < 2 * hg, middle, low))
        stats = jnp.where(lane < 3 * hg, stats, 0.0)
        slabs.append(jnp.concatenate([mixed, stats], axis=1).reshape(n, cd, gw + 128))
        if half >= 2 and g == 0:
            pump(2)
    if groups * cd < slot:
        slabs.append(jnp.zeros((n, slot - groups * cd, gw + 128), F32))
    bo[...] = jnp.concatenate(slabs, axis=1).astype(BF16)
    br[me] = bo[me]
    for j in range(1, n):
        exchange(bo, br, b_send, b_recv, j, True).start()

    for hop in range(3, half + 1):
        pump(hop)
    for index, offset, j in shared:
        share(index, offset, j, False).wait_recv()

    before = []
    for g in range(groups):
        cols = slice(g * gw, (g + 1) * gw)
        root_keys = kroot[:, :, cols].reshape(n * block, gw)
        root_values = vroot[:, :, cols].reshape(n * block, gw)
        peaks, sums, weighted = attend_long(stacked[g], root_keys, root_values, None, min(128, hg * rows))
        lpeaks, lsums, lweighted = local_states[g]
        level = jnp.zeros((rows, gw), F32)
        amount = jnp.zeros((rows, gw), F32)
        mixed = jnp.zeros((rows, gw), F32)
        for h in range(hg):
            at = slice(h * rows, (h + 1) * rows)
            top = jnp.maximum(peaks[at], lpeaks[h])
            one = jnp.exp2((peaks[at] - top) * SCALE)
            two = jnp.exp2((lpeaks[h] - top) * SCALE)
            level = jnp.where(col_head == h, top * SCALE, level)
            amount = jnp.where(col_head == h, one * sums[at] + two * lsums[h], amount)
            mixed = jnp.where(col_head == h, one * weighted[at] + two * lweighted[at], mixed)
        before.append((level, amount, mixed))

    group_l, item_l, draft_l = slot_parts((rows, total), 1)
    take = (dot_t(target, spread) > 0.5) & (order_col == item_l) & (
        lax.rem(iota((rows, total), 0), drafts) == draft_l
    )
    takes = [jnp.where(take & (group_l == g), 1.0, 0.0).astype(BF16) for g in range(groups)]
    loads[5].wait()

    for j in range(1, n):
        exchange(bo, br, b_send, b_recv, j, False).wait_recv()
    flat = br[...].reshape(total, gw + 128)
    heads = []
    for g in range(groups):
        got = dot(takes[g], flat)
        stats = got[:, gw:]
        level, amount, mixed = before[g]
        other = jnp.zeros((rows, gw), F32)
        for h in range(hg):
            joined = (
                stats[:, h : h + 1]
                + stats[:, hg + h : hg + h + 1]
                + stats[:, 2 * hg + h : 2 * hg + h + 1]
            )
            other = jnp.where(col_head == h, joined, other)
        top = jnp.maximum(level, other)
        one = jnp.exp2(level - top)
        two = jnp.exp2(other - top)
        heads.append(((one * mixed + two * got[:, :gw]) / (one * amount + two)).astype(BF16))
    attention = heads[0] if groups == 1 else jnp.concatenate(heads, axis=1)
    ow = out_ref.shape[1]

    def reduce_copy(j, outgoing):
        there = lax.rem(tn + j, nt)
        here = tn if outgoing else lax.rem(tn + nt - j, nt)
        return pltpu.make_async_remote_copy(
            src_ref=tb.at[there], dst_ref=tr.at[here],
            send_sem=t_send.at[j], recv_sem=t_recv.at[j],
            device_id=(me, there), device_id_type=MESH,
        )

    def term(t):
        return dot(attention, wout_ref[:, pl.ds(pl.multiple_of(t * ow, ow), ow)])

    for j in range(1, nt):
        there = lax.rem(tn + j, nt)
        tb[there] = term(there).astype(BF16)
        reduce_copy(j, True).start()
    in_use = lax.rem(iota((rows, 1), 0), drafts).astype(F32) < new_count
    result = term(tn)
    for copy in sent:
        copy.wait_send()
    for j in range(1, n):
        exchange(oq, aq, q_send, q_recv, j, True).wait_send()
        exchange(bo, br, b_send, b_recv, j, True).wait_send()
    for j in range(1, nt):
        reduce_copy(j, False).wait_recv()
        result = result + tr[lax.rem(tn + nt - j, nt)].astype(F32)
    out_ref[...] = jnp.where(in_use, result, 0.0).astype(BF16)
    for j in range(1, nt):
        reduce_copy(j, True).wait_send()


def local(
    n, nt,
    tokens, norm_gain, w_qkv, w_out, root_kv, branch_kv, leaf_kv,
    branch, node_owner, branch_len, leaf_len, new_count,
):
    rows, depth = tokens.shape
    requests = branch.shape[0]
    drafts = rows // requests
    nodes = node_owner.shape[0]
    width = w_out.shape[0]
    ow = w_out.shape[1] // nt
    cap = max(2, 2 * requests // nodes)
    gw = min(width, 256)
    slot = max(16, width // gw * cap * drafts)
    block = root_kv.shape[0]
    span = branch_kv.shape[1]
    leaf_rows = leaf_kv.shape[0] * leaf_kv.shape[1]
    half = n // 4
    long_rows = gw // HD * max(n * cap * drafts, rows)
    longest = max(span, n * block)
    vmem = pl.BlockSpec(memory_space=pltpu.VMEM)
    hbm = pl.BlockSpec(memory_space=pl.ANY)
    dma = pltpu.SemaphoreType.DMA
    return pl.pallas_call(
        functools.partial(kernel, n, nt, drafts, cap),
        out_shape=jax.ShapeDtypeStruct((rows, ow), BF16),
        in_specs=[vmem, vmem, hbm, hbm, vmem, hbm, hbm] + [vmem] * 5,
        out_specs=vmem,
        scratch_shapes=[
            pltpu.VMEM((3, depth, width), BF16),
            pltpu.VMEM(w_out.shape, BF16),
            pltpu.VMEM((span, 2, width), BF16),
            pltpu.VMEM((leaf_rows, 2, width), BF16),
            pltpu.VMEM((n, block, width), BF16),
            pltpu.VMEM((n, block, width), BF16),
            pltpu.VMEM((span, width), BF16),
            pltpu.VMEM((span, width), BF16),
            pltpu.VMEM((leaf_rows + rows, width), BF16),
            pltpu.VMEM((leaf_rows + rows, width), BF16),
            pltpu.VMEM((n, slot, gw), BF16),
            pltpu.VMEM((n, slot, gw), BF16),
            pltpu.VMEM((n, slot, gw + 128), BF16),
            pltpu.VMEM((n, slot, gw + 128), BF16),
            pltpu.VMEM((nt, rows, ow), BF16),
            pltpu.VMEM((nt, rows, ow), BF16),
            pltpu.VMEM((long_rows, longest), F32),
            pltpu.VMEM((long_rows, longest), BF16),
            pltpu.VMEM((long_rows, 128), F32),
            pltpu.VMEM((long_rows, 128), F32),
            pltpu.VMEM((n, slot, gw), F32),
            dma((6,)),
            dma((2, half + 1, 2)),
            dma((2, half + 1, 2)),
            dma((2 * half + 1, 2)),
            dma((2 * half + 1, 2)),
            dma((n,)),
            dma((n,)),
            dma((n,)),
            dma((n,)),
            dma((nt,)),
            dma((nt,)),
        ],
        compiler_params=pltpu.CompilerParams(
            collective_id=0, has_side_effects=True, vmem_limit_bytes=58 << 20
        ),
    )(
        tokens,
        norm_gain.reshape(1, -1),
        jnp.transpose(w_qkv, (1, 0, 2)),
        w_out,
        root_kv,
        branch_kv.reshape(span, 2, width),
        leaf_kv.reshape(leaf_rows, 2, width),
        branch.reshape(1, requests),
        node_owner.reshape(1, nodes),
        branch_len.reshape(1, nodes),
        leaf_len.reshape(1, requests),
        new_count.reshape(1, requests),
    )


def solution(mesh):
    placed = (
        P("req", None),
        P(),
        P(None, None, "tensor"),
        P("tensor", None),
        P("req", None, "tensor"),
        P("req", None, None, "tensor"),
        P("req", None, None, "tensor"),
        P("req", None),
        P(),
        P(),
        P("req"),
        P("req"),
    )
    return jax.shard_map(
        functools.partial(local, mesh.shape["req"], mesh.shape["tensor"]),
        mesh=mesh, in_specs=placed, out_specs=P("req", "tensor"), check_vma=False,
    )
```

```python
import functools
import math

import jax
import jax.numpy as jnp
from jax import lax
from jax.experimental import pallas as pl
from jax.experimental.pallas import tpu as pltpu
from jax.sharding import PartitionSpec as P

HD = 64
MESH = pl.DeviceIdType.MESH
F32 = jnp.float32
BF16 = jnp.bfloat16
SCALE = HD ** (-0.5) * math.log2(math.e)
LOG2E = math.log2(math.e)


def iota(shape, dim):
    return lax.broadcasted_iota(jnp.int32, shape, dim)


def div(a, by):
    return a >> (by.bit_length() - 1) if by & (by - 1) == 0 else lax.div(a, by)


def rem(a, by):
    return a & (by - 1) if by & (by - 1) == 0 else lax.rem(a, by)


def dot(a, b):
    return jnp.dot(a, b, preferred_element_type=F32)


def dot_t(a, b):
    return lax.dot_general(a, b, (((1,), (1,)), ((), ())), preferred_element_type=F32)


def kernel(
    n, nt, drafts, cap,
    tok_ref, gain_ref, w_hbm, wout_hbm, root_ref, bkv_hbm, leaf_hbm,
    branch_ref, owner_ref, blen_ref, llen_ref, newc_ref,
    out_ref,
    w_ref, wout_ref, braw, lraw, kvroot, kbr, vbr, kloc, vloc,
    oq, aq, bo, br, tb, tr, sbuf, pbuf, peak_buf, sum_buf, asked,
    local_sem, root_send, ring_recv, sib_recv,
    q_send, q_recv, b_send, b_recv, t_send, t_recv,
):
    rows = tok_ref.shape[0]
    requests = rows // drafts
    width = wout_hbm.shape[0]
    gw = min(width, 256)
    hg = gw // HD
    groups = width // gw
    cd = cap * drafts
    slot = oq.shape[1]
    span = bkv_hbm.shape[0]
    leaf_span = leaf_hbm.shape[0] // requests
    block = root_ref.shape[0]
    chips = n // 2
    half = chips // 2
    me = lax.axis_index("req")
    tn = lax.axis_index("tensor")

    loads = [pltpu.make_async_copy(w_hbm.at[j], w_ref.at[j], local_sem.at[j]) for j in range(3)]
    loads.append(pltpu.make_async_copy(bkv_hbm, braw, local_sem.at[3]))
    loads.append(pltpu.make_async_copy(leaf_hbm, lraw, local_sem.at[4]))
    loads.append(pltpu.make_async_copy(wout_hbm, wout_ref, local_sem.at[5]))
    for load in loads:
        load.start()

    barrier = pltpu.get_barrier_semaphore()

    def greet(j, carry):
        pl.semaphore_signal(
            barrier, inc=1, device_id=(lax.rem(me + j, n), tn), device_id_type=MESH
        )
        return carry

    lax.fori_loop(1, n, greet, 0)
    for j in range(1, nt):
        pl.semaphore_signal(
            barrier, inc=1, device_id=(me, lax.rem(tn + j, nt)), device_id_type=MESH
        )

    def splitter(count):
        pick = iota((2 * count, 2 * count), 0)
        col = iota((2 * count, 2 * count), 1)
        source = jnp.where(pick < count, 2 * pick, 2 * (pick - count) + 1)
        return (col == source).astype(BF16)

    def split_rows(chosen, raw):
        count = raw.shape[0] // 2
        parted = dot(chosen, raw).astype(BF16)
        return parted[:count], parted[count:]

    own_k, own_v = split_rows(splitter(block), root_ref.reshape(2 * block, width)[...])
    kvroot[me, 0] = own_k
    kvroot[me, 1] = own_v

    core = lax.rem(me, 2)
    chip = lax.div(me, 2)
    zc = lax.div(chip, 2)
    xc = lax.rem(chip, 2)
    place = (1 - xc) * zc + xc * (2 * half - 1 - zc)

    def device_at(position):
        q = lax.rem(position + 2 * chips, chips)
        xq = lax.div(q, half)
        zq = (1 - xq) * q + xq * (2 * half - 1 - q)
        return (zq * 2 + xq) * 2 + core

    sibling = me + 1 - 2 * core

    def ring(direction, hop, outgoing):
        sign = 1 - 2 * direction
        origin = device_at(place - sign * (hop - 1 if outgoing else hop))
        part = kvroot.at[origin] if hop < half else kvroot.at[origin, direction]
        return pltpu.make_async_remote_copy(
            src_ref=part, dst_ref=part,
            send_sem=root_send.at[0], recv_sem=ring_recv.at[direction, hop],
            device_id=(device_at(place + sign), tn), device_id_type=MESH,
        )

    def share(index, offset, outgoing):
        origin = device_at(place + offset)
        if not outgoing:
            origin = origin + 1 - 2 * core
        return pltpu.make_async_remote_copy(
            src_ref=kvroot.at[origin], dst_ref=kvroot.at[origin],
            send_sem=root_send.at[0], recv_sem=sib_recv.at[index],
            device_id=(sibling, tn), device_id_type=MESH,
        )

    shared = [(0, 0)]
    shared += [(k, -k) for k in range(1, half + 1)]
    shared += [(half + k, k) for k in range(1, half)]

    def pump(hop):
        for direction in range(2):
            ring(direction, hop, False).wait_recv()
            if hop < half:
                ring(direction, hop + 1, True).start()
                share(direction * half + hop, hop * (2 * direction - 1), True).start()
        if hop == half:
            share(half, -half, True).start()

    pl.semaphore_wait(barrier, n - 1 + nt - 1)
    for direction in range(2):
        ring(direction, 1, True).start()
    share(0, 0, True).start()

    floats = tok_ref[...].astype(F32)
    mean = jnp.mean(floats * floats, axis=1, keepdims=True)
    normed = (floats * lax.rsqrt(mean + 1e-05) * gain_ref[...]).astype(BF16)
    loads[0].wait()
    queries = dot(normed, w_ref[0]).astype(BF16)

    row_req = div(iota((rows, requests), 0), drafts)
    at_req = row_req == iota((rows, requests), 1)

    def per_row(values):
        return jnp.sum(jnp.where(at_req, values.astype(F32), 0.0), axis=1, keepdims=True)

    node_of = per_row(branch_ref[...])
    chosen = (node_of == iota((rows, n), 1).astype(F32)).astype(BF16)
    owners = (owner_ref[...] == iota((n, n), 0)).astype(BF16)
    target = dot_t(chosen, owners).astype(BF16)
    target_t = dot_t(owners, chosen).astype(BF16)
    same = dot_t(target, target)
    ri, rj = iota((rows, rows), 0), iota((rows, rows), 1)
    qi, qj = div(ri, drafts), div(rj, drafts)
    first_j = rem(rj, drafts) == 0
    first_i = rem(ri, drafts) == 0
    order_col = jnp.sum(jnp.where((qj < qi) & first_j, same, 0.0), axis=1, keepdims=True)
    order_row = jnp.sum(jnp.where((qi < qj) & first_i, same, 0.0), axis=0, keepdims=True)
    total = n * slot
    spread = (div(iota((total, n), 0), slot) == iota((total, n), 1)).astype(BF16)

    def slot_parts(shape, dim):
        inner = rem(iota(shape, dim), slot)
        item = rem(inner, cd)
        return div(inner, cd), div(item, drafts).astype(F32), rem(item, drafts)

    group_k, item_k, draft_k = slot_parts((total, rows), 0)
    put = (dot(spread, target_t) > 0.5) & (order_row == item_k) & (
        rem(iota((total, rows), 1), drafts) == draft_k
    )
    packed = jnp.zeros((total, gw), F32)
    for g in range(groups):
        mine = jnp.where(put & (group_k == g), 1.0, 0.0).astype(BF16)
        packed = packed + dot(mine, queries[:, g * gw : (g + 1) * gw])
    oq[...] = packed.astype(BF16).reshape(n, slot, gw)
    aq[me] = oq[me]

    def exchange(source, landing, send_sem, recv_sem, j):
        there = lax.rem(me + j, n)
        return pltpu.make_async_remote_copy(
            src_ref=source.at[there], dst_ref=landing.at[me],
            send_sem=send_sem.at[0], recv_sem=recv_sem.at[0],
            device_id=(there, tn), device_id_type=MESH,
        )

    def of_all(source, landing, send_sem, recv_sem):
        return pltpu.make_async_remote_copy(
            src_ref=source.at[pl.ds(0, n - 1)], dst_ref=landing.at[pl.ds(0, n - 1)],
            send_sem=send_sem.at[0], recv_sem=recv_sem.at[0],
            device_id=(lax.rem(me + 1, n), tn), device_id_type=MESH,
        )

    for j in range(1, n):
        exchange(oq, aq, q_send, q_recv, j).start()
    pump(1)

    loads[1].wait()
    own_keys = dot(normed, w_ref[1]).astype(BF16)
    loads[2].wait()
    own_values = dot(normed, w_ref[2]).astype(BF16)

    loads[3].wait()
    piece = min(128, span)
    braw_rows = braw.reshape(2 * span, width)

    branch_pick = splitter(piece)

    def part_branch(b, carry):
        raw = braw_rows[pl.ds(pl.multiple_of(2 * piece * b, 2 * piece), 2 * piece), :]
        k_part, v_part = split_rows(branch_pick, raw)
        at = pl.ds(pl.multiple_of(piece * b, piece), piece)
        kbr[at, :] = k_part
        vbr[at, :] = v_part
        return carry

    lax.fori_loop(0, span // piece, part_branch, 0)

    col_head = div(iota((1, gw), 1), HD)

    def stack(part):
        return jnp.concatenate(
            [jnp.where(col_head == h, part, 0.0) for h in range(hg)], axis=0
        ).astype(BF16)

    def attend(scores, mask, values):
        peaks, sums, weights = [], [], []
        for s, keep in zip(scores, mask):
            if keep is not None:
                s = jnp.where(keep, s, -1e30)
            peak = jnp.max(s, axis=1, keepdims=True)
            w = jnp.exp2((s - peak) * SCALE)
            peaks.append(peak)
            sums.append(jnp.sum(w, axis=1, keepdims=True))
            weights.append(w.astype(BF16))
        weighted = dot(jnp.concatenate(weights, axis=0), values)
        return peaks, sums, weighted

    def attend_long(stacked_rows, keys_of, values_of, keep, step):
        amount_of, length = stacked_rows.shape[0], keys_of.shape[0]
        sbuf[:amount_of, :length] = dot_t(stacked_rows, keys_of)

        def some(c, carry):
            for part in range(0, step, 32):
                at = pl.ds(pl.multiple_of(c * step + part, 32), 32)
                s = sbuf[at, :length]
                if keep is not None:
                    s = jnp.where(keep, s, -1e30)
                peak = jnp.max(s, axis=1, keepdims=True)
                w = jnp.exp2((s - peak) * SCALE)
                peak_buf[at, :] = jnp.broadcast_to(peak, (32, 128))
                sum_buf[at, :] = jnp.broadcast_to(jnp.sum(w, axis=1, keepdims=True), (32, 128))
                pbuf[at, :length] = w.astype(BF16)
            return carry

        lax.fori_loop(0, amount_of // step, some, 0)
        weighted = dot(pbuf[:amount_of, :length], values_of)
        return peak_buf[:amount_of, :1], sum_buf[:amount_of, :1], weighted

    loads[4].wait()
    leaf_rows = requests * leaf_span
    lpiece = min(128, leaf_rows)
    lraw_rows = lraw.reshape(2 * leaf_rows, width)

    leaf_pick = branch_pick if lpiece == piece else splitter(lpiece)

    def part_leaf(b, carry):
        raw = lraw_rows[pl.ds(pl.multiple_of(2 * lpiece * b, 2 * lpiece), 2 * lpiece), :]
        k_part, v_part = split_rows(leaf_pick, raw)
        at = pl.ds(pl.multiple_of(lpiece * b, lpiece), lpiece)
        kloc[at, :] = k_part
        vloc[at, :] = v_part
        return carry

    lax.fori_loop(0, leaf_rows // lpiece, part_leaf, 0)
    kloc[pl.ds(leaf_rows, rows), :] = own_keys
    vloc[pl.ds(leaf_rows, rows), :] = own_values
    keys = leaf_rows + rows
    leaf_len = per_row(llen_ref[...])
    new_count = per_row(newc_ref[...])
    ki, kj = iota((rows, keys), 0), iota((rows, keys), 1)
    own_j = kj - leaf_rows
    draft_j = rem(jnp.maximum(own_j, 0), drafts)
    in_leaf = (
        (div(kj, leaf_span) == div(ki, drafts))
        & (rem(kj, leaf_span).astype(F32) < leaf_len)
    )
    in_own = (
        (div(jnp.maximum(own_j, 0), drafts) == div(ki, drafts))
        & (draft_j <= rem(ki, drafts))
        & (draft_j.astype(F32) < new_count)
    )
    local_keep = ((kj < leaf_rows) & in_leaf) | ((kj >= leaf_rows) & in_own)
    stacked = [stack(queries[:, g * gw : (g + 1) * gw].astype(F32)) for g in range(groups)]
    local_states = []
    for g in range(groups):
        cols = slice(g * gw, (g + 1) * gw)
        scores = dot_t(stacked[g], kloc[:, cols])
        pieces = [scores[h * rows : (h + 1) * rows] for h in range(hg)]
        local_states.append(attend(pieces, [local_keep] * hg, vloc[:, cols]))

    if half >= 2:
        pump(2)

    of_all(oq, aq, q_send, q_recv).wait_recv()
    asked[...] = aq[...].astype(F32)
    owned = jnp.sum(
        jnp.where(owner_ref[...] == me, blen_ref[...], 0).astype(F32), axis=1, keepdims=True
    )
    usable = iota((1, span), 1).astype(F32) < owned
    count = n * cd
    lane = iota((1, 128), 1)
    slabs = []
    for g in range(groups):
        part = asked[:, g * cd : (g + 1) * cd, :].reshape(count, gw)
        cols = slice(g * gw, (g + 1) * gw)
        peaks, sums, weighted = attend_long(stack(part), kbr[:, cols], vbr[:, cols], usable, 128)
        inverse = 1.0 / sums
        level = peaks * SCALE + jnp.log(sums) * LOG2E
        mixed = jnp.zeros((count, gw), F32)
        levels = jnp.zeros((count, 128), F32)
        for h in range(hg):
            at = slice(h * count, (h + 1) * count)
            mixed = jnp.where(col_head == h, weighted[at] * inverse[at], mixed)
            levels = jnp.where(rem(lane, hg) == h, level[at], levels)
        high = levels.astype(BF16).astype(F32)
        middle = (levels - high).astype(BF16).astype(F32)
        low = levels - high - middle
        stats = jnp.where(lane < hg, high, jnp.where(lane < 2 * hg, middle, low))
        stats = jnp.where(lane < 3 * hg, stats, 0.0)
        slabs.append(jnp.concatenate([mixed, stats], axis=1).reshape(n, cd, gw + 128))
        if half >= 3 and g == 0:
            pump(3)
    if groups * cd < slot:
        slabs.append(jnp.zeros((n, slot - groups * cd, gw + 128), F32))
    bo[...] = jnp.concatenate(slabs, axis=1).astype(BF16)
    br[me] = bo[me]
    for j in range(1, n):
        exchange(bo, br, b_send, b_recv, j).start()

    for hop in range(4, half + 1):
        pump(hop)
    for index, offset in shared:
        share(index, offset, False).wait_recv()

    before = []
    for g in range(groups):
        cols = slice(g * gw, (g + 1) * gw)
        root_keys = kvroot[:, 0, :, cols].reshape(n * block, gw)
        root_values = kvroot[:, 1, :, cols].reshape(n * block, gw)
        peaks, sums, weighted = attend_long(stacked[g], root_keys, root_values, None, min(128, hg * rows))
        lpeaks, lsums, lweighted = local_states[g]
        level = jnp.zeros((rows, gw), F32)
        amount = jnp.zeros((rows, gw), F32)
        mixed = jnp.zeros((rows, gw), F32)
        for h in range(hg):
            at = slice(h * rows, (h + 1) * rows)
            top = jnp.maximum(peaks[at], lpeaks[h])
            one = jnp.exp2((peaks[at] - top) * SCALE)
            two = jnp.exp2((lpeaks[h] - top) * SCALE)
            level = jnp.where(col_head == h, top * SCALE, level)
            amount = jnp.where(col_head == h, one * sums[at] + two * lsums[h], amount)
            mixed = jnp.where(col_head == h, one * weighted[at] + two * lweighted[at], mixed)
        before.append((level, amount, mixed))

    group_l, item_l, draft_l = slot_parts((rows, total), 1)
    take = (dot_t(target, spread) > 0.5) & (order_col == item_l) & (
        rem(iota((rows, total), 0), drafts) == draft_l
    )
    takes = [jnp.where(take & (group_l == g), 1.0, 0.0).astype(BF16) for g in range(groups)]
    loads[5].wait()

    of_all(bo, br, b_send, b_recv).wait_recv()
    flat = br[...].reshape(total, gw + 128)
    heads = []
    for g in range(groups):
        got = dot(takes[g], flat)
        stats = got[:, gw:]
        level, amount, mixed = before[g]
        other = jnp.zeros((rows, gw), F32)
        for h in range(hg):
            joined = (
                stats[:, h : h + 1]
                + stats[:, hg + h : hg + h + 1]
                + stats[:, 2 * hg + h : 2 * hg + h + 1]
            )
            other = jnp.where(col_head == h, joined, other)
        top = jnp.maximum(level, other)
        one = jnp.exp2(level - top)
        two = jnp.exp2(other - top)
        heads.append(((one * mixed + two * got[:, :gw]) / (one * amount + two)).astype(BF16))
    attention = heads[0] if groups == 1 else jnp.concatenate(heads, axis=1)
    ow = out_ref.shape[1]

    def reduce_copy(j, outgoing):
        there = lax.rem(tn + j, nt)
        here = tn if outgoing else lax.rem(tn + nt - j, nt)
        return pltpu.make_async_remote_copy(
            src_ref=tb.at[there], dst_ref=tr.at[here],
            send_sem=t_send.at[j], recv_sem=t_recv.at[j],
            device_id=(me, there), device_id_type=MESH,
        )

    def term(t):
        return dot(attention, wout_ref[:, pl.ds(pl.multiple_of(t * ow, ow), ow)])

    for j in range(1, nt):
        there = lax.rem(tn + j, nt)
        tb[there] = term(there).astype(BF16)
        reduce_copy(j, True).start()
    in_use = rem(iota((rows, 1), 0), drafts).astype(F32) < new_count
    result = term(tn)
    of_all(kvroot, kvroot, root_send, root_send).wait_send()
    of_all(oq, aq, q_send, q_recv).wait_send()
    of_all(bo, br, b_send, b_recv).wait_send()
    for j in range(1, nt):
        reduce_copy(j, False).wait_recv()
        result = result + tr[lax.rem(tn + nt - j, nt)].astype(F32)
    out_ref[...] = jnp.where(in_use, result, 0.0).astype(BF16)
    for j in range(1, nt):
        reduce_copy(j, True).wait_send()


def local(
    n, nt,
    tokens, norm_gain, w_qkv, w_out, root_kv, branch_kv, leaf_kv,
    branch, node_owner, branch_len, leaf_len, new_count,
):
    rows, depth = tokens.shape
    requests = branch.shape[0]
    drafts = rows // requests
    nodes = node_owner.shape[0]
    width = w_out.shape[0]
    ow = w_out.shape[1] // nt
    cap = max(2, 2 * requests // nodes)
    gw = min(width, 256)
    slot = max(16, width // gw * cap * drafts)
    block = root_kv.shape[0]
    span = branch_kv.shape[1]
    leaf_rows = leaf_kv.shape[0] * leaf_kv.shape[1]
    half = n // 4
    long_rows = gw // HD * max(n * cap * drafts, rows)
    longest = max(span, n * block)
    vmem = pl.BlockSpec(memory_space=pltpu.VMEM)
    hbm = pl.BlockSpec(memory_space=pl.ANY)
    dma = pltpu.SemaphoreType.DMA
    return pl.pallas_call(
        functools.partial(kernel, n, nt, drafts, cap),
        out_shape=jax.ShapeDtypeStruct((rows, ow), BF16),
        in_specs=[vmem, vmem, hbm, hbm, vmem, hbm, hbm] + [vmem] * 5,
        out_specs=vmem,
        scratch_shapes=[
            pltpu.VMEM((3, depth, width), BF16),
            pltpu.VMEM(w_out.shape, BF16),
            pltpu.VMEM((span, 2, width), BF16),
            pltpu.VMEM((leaf_rows, 2, width), BF16),
            pltpu.VMEM((n, 2, block, width), BF16),
            pltpu.VMEM((span, width), BF16),
            pltpu.VMEM((span, width), BF16),
            pltpu.VMEM((leaf_rows + rows, width), BF16),
            pltpu.VMEM((leaf_rows + rows, width), BF16),
            pltpu.VMEM((n, slot, gw), BF16),
            pltpu.VMEM((n, slot, gw), BF16),
            pltpu.VMEM((n, slot, gw + 128), BF16),
            pltpu.VMEM((n, slot, gw + 128), BF16),
            pltpu.VMEM((nt, rows, ow), BF16),
            pltpu.VMEM((nt, rows, ow), BF16),
            pltpu.VMEM((long_rows, longest), F32),
            pltpu.VMEM((long_rows, longest), BF16),
            pltpu.VMEM((long_rows, 128), F32),
            pltpu.VMEM((long_rows, 128), F32),
            pltpu.VMEM((n, slot, gw), F32),
            dma((6,)),
            dma((1,)),
            dma((2, half + 1)),
            dma((2 * half,)),
            dma((1,)),
            dma((1,)),
            dma((1,)),
            dma((1,)),
            dma((nt,)),
            dma((nt,)),
        ],
        compiler_params=pltpu.CompilerParams(
            collective_id=0, has_side_effects=True, vmem_limit_bytes=58 << 20
        ),
    )(
        tokens,
        norm_gain.reshape(1, -1),
        jnp.transpose(w_qkv, (1, 0, 2)),
        w_out,
        root_kv,
        branch_kv.reshape(span, 2, width),
        leaf_kv.reshape(leaf_rows, 2, width),
        branch.reshape(1, requests),
        node_owner.reshape(1, nodes),
        branch_len.reshape(1, nodes),
        leaf_len.reshape(1, requests),
        new_count.reshape(1, requests),
    )


def solution(mesh):
    placed = (
        P("req", None),
        P(),
        P(None, None, "tensor"),
        P("tensor", None),
        P("req", None, "tensor"),
        P("req", None, None, "tensor"),
        P("req", None, None, "tensor"),
        P("req", None),
        P(),
        P(),
        P("req"),
        P("req"),
    )
    return jax.shard_map(
        functools.partial(local, mesh.shape["req"], mesh.shape["tensor"]),
        mesh=mesh, in_specs=placed, out_specs=P("req", "tensor"), check_vma=False,
    )
```

```python
import functools
import math

import jax
import jax.numpy as jnp
from jax import lax
from jax.experimental import pallas as pl
from jax.experimental.pallas import tpu as pltpu
from jax.sharding import PartitionSpec as P

HD = 64
MESH = pl.DeviceIdType.MESH
F32 = jnp.float32
BF16 = jnp.bfloat16
SCALE = HD ** (-0.5) * math.log2(math.e)
LOG2E = math.log2(math.e)


def iota(shape, dim):
    return lax.broadcasted_iota(jnp.int32, shape, dim)


def div(a, by):
    return a >> (by.bit_length() - 1) if by & (by - 1) == 0 else lax.div(a, by)


def rem(a, by):
    return a & (by - 1) if by & (by - 1) == 0 else lax.rem(a, by)


def dot(a, b):
    return jnp.dot(a, b, preferred_element_type=F32)


def dot_t(a, b):
    return lax.dot_general(a, b, (((1,), (1,)), ((), ())), preferred_element_type=F32)


def kernel(
    n, nt, drafts, cap,
    tok_ref, gain_ref, w_hbm, wout_hbm, root_ref, bkv_hbm, leaf_hbm,
    branch_ref, owner_ref, blen_ref, llen_ref, newc_ref,
    out_ref,
    w_ref, wout_ref, braw, lraw, kvroot, kbr, vbr, kloc, vloc,
    oq, aq, bo, br, tb, tr, sbuf, pbuf, peak_buf, sum_buf, asked,
    local_sem, root_send, ring_recv, sib_recv,
    q_send, q_recv, b_send, b_recv, t_send, t_recv,
):
    rows = tok_ref.shape[0]
    requests = rows // drafts
    width = wout_hbm.shape[0]
    gw = min(width, 256)
    hg = gw // HD
    groups = width // gw
    cd = cap * drafts
    slot = oq.shape[1]
    span = bkv_hbm.shape[0]
    leaf_span = leaf_hbm.shape[0] // requests
    block = root_ref.shape[0]
    chips = n // 2
    half = chips // 2
    me = lax.axis_index("req")
    tn = lax.axis_index("tensor")

    loads = [pltpu.make_async_copy(w_hbm.at[j], w_ref.at[j], local_sem.at[j]) for j in range(3)]
    loads.append(pltpu.make_async_copy(bkv_hbm, braw, local_sem.at[3]))
    loads.append(pltpu.make_async_copy(leaf_hbm, lraw, local_sem.at[4]))
    loads.append(pltpu.make_async_copy(wout_hbm, wout_ref, local_sem.at[5]))
    for load in loads[:3]:
        load.start()

    barrier = pltpu.get_barrier_semaphore()

    def greet(j, carry):
        pl.semaphore_signal(
            barrier, inc=1, device_id=(lax.rem(me + j, n), tn), device_id_type=MESH
        )
        return carry

    lax.fori_loop(1, n, greet, 0)
    for j in range(1, nt):
        pl.semaphore_signal(
            barrier, inc=1, device_id=(me, lax.rem(tn + j, nt)), device_id_type=MESH
        )

    def splitter(count):
        pick = iota((2 * count, 2 * count), 0)
        col = iota((2 * count, 2 * count), 1)
        source = jnp.where(pick < count, 2 * pick, 2 * (pick - count) + 1)
        return (col == source).astype(BF16)

    def split_rows(chosen, raw):
        count = raw.shape[0] // 2
        parted = dot(chosen, raw).astype(BF16)
        return parted[:count], parted[count:]

    own_k, own_v = split_rows(splitter(block), root_ref.reshape(2 * block, width)[...])
    kvroot[me, 0] = own_k
    kvroot[me, 1] = own_v

    core = lax.rem(me, 2)
    chip = lax.div(me, 2)
    zc = lax.div(chip, 2)
    xc = lax.rem(chip, 2)
    place = (1 - xc) * zc + xc * (2 * half - 1 - zc)

    def device_at(position):
        q = lax.rem(position + 2 * chips, chips)
        xq = lax.div(q, half)
        zq = (1 - xq) * q + xq * (2 * half - 1 - q)
        return (zq * 2 + xq) * 2 + core

    sibling = me + 1 - 2 * core

    def ring(direction, hop, outgoing):
        sign = 1 - 2 * direction
        origin = device_at(place - sign * (hop - 1 if outgoing else hop))
        part = kvroot.at[origin] if hop < half else kvroot.at[origin, direction]
        return pltpu.make_async_remote_copy(
            src_ref=part, dst_ref=part,
            send_sem=root_send.at[0], recv_sem=ring_recv.at[direction, hop],
            device_id=(device_at(place + sign), tn), device_id_type=MESH,
        )

    def share(index, offset, outgoing):
        origin = device_at(place + offset)
        if not outgoing:
            origin = origin + 1 - 2 * core
        return pltpu.make_async_remote_copy(
            src_ref=kvroot.at[origin], dst_ref=kvroot.at[origin],
            send_sem=root_send.at[0], recv_sem=sib_recv.at[index],
            device_id=(sibling, tn), device_id_type=MESH,
        )

    shared = [(0, 0)]
    shared += [(k, -k) for k in range(1, half + 1)]
    shared += [(half + k, k) for k in range(1, half)]

    def pump(hop):
        for direction in range(2):
            ring(direction, hop, False).wait_recv()
            if hop < half:
                ring(direction, hop + 1, True).start()
                share(direction * half + hop, hop * (2 * direction - 1), True).start()
        if hop == half:
            share(half, -half, True).start()

    pl.semaphore_wait(barrier, n - 1 + nt - 1)
    for direction in range(2):
        ring(direction, 1, True).start()
    share(0, 0, True).start()

    floats = tok_ref[...].astype(F32)
    mean = jnp.mean(floats * floats, axis=1, keepdims=True)
    normed = (floats * lax.rsqrt(mean + 1e-05) * gain_ref[...]).astype(BF16)
    loads[0].wait()
    for load in loads[3:]:
        load.start()
    queries = dot(normed, w_ref[0]).astype(BF16)

    row_req = div(iota((rows, requests), 0), drafts)
    at_req = row_req == iota((rows, requests), 1)

    def per_row(values):
        return jnp.sum(jnp.where(at_req, values.astype(F32), 0.0), axis=1, keepdims=True)

    node_of = per_row(branch_ref[...])
    chosen = (node_of == iota((rows, n), 1).astype(F32)).astype(BF16)
    owners = (owner_ref[...] == iota((n, n), 0)).astype(BF16)
    target = dot_t(chosen, owners).astype(BF16)
    target_t = dot_t(owners, chosen).astype(BF16)
    same = dot_t(target, target)
    ri, rj = iota((rows, rows), 0), iota((rows, rows), 1)
    qi, qj = div(ri, drafts), div(rj, drafts)
    first_j = rem(rj, drafts) == 0
    first_i = rem(ri, drafts) == 0
    order_col = jnp.sum(jnp.where((qj < qi) & first_j, same, 0.0), axis=1, keepdims=True)
    order_row = jnp.sum(jnp.where((qi < qj) & first_i, same, 0.0), axis=0, keepdims=True)
    total = n * slot
    spread = (div(iota((total, n), 0), slot) == iota((total, n), 1)).astype(BF16)

    def slot_parts(shape, dim):
        inner = rem(iota(shape, dim), slot)
        item = rem(inner, cd)
        return div(inner, cd), div(item, drafts).astype(F32), rem(item, drafts)

    group_k, item_k, draft_k = slot_parts((total, rows), 0)
    put = (dot(spread, target_t) > 0.5) & (order_row == item_k) & (
        rem(iota((total, rows), 1), drafts) == draft_k
    )
    packed = jnp.zeros((total, gw), F32)
    for g in range(groups):
        mine = jnp.where(put & (group_k == g), 1.0, 0.0).astype(BF16)
        packed = packed + dot(mine, queries[:, g * gw : (g + 1) * gw])
    oq[...] = packed.astype(BF16).reshape(n, slot, gw)
    aq[me] = oq[me]

    def exchange(source, landing, send_sem, recv_sem, j):
        there = lax.rem(me + j, n)
        return pltpu.make_async_remote_copy(
            src_ref=source.at[there], dst_ref=landing.at[me],
            send_sem=send_sem.at[0], recv_sem=recv_sem.at[0],
            device_id=(there, tn), device_id_type=MESH,
        )

    def of_all(source, landing, send_sem, recv_sem):
        return pltpu.make_async_remote_copy(
            src_ref=source.at[pl.ds(0, n - 1)], dst_ref=landing.at[pl.ds(0, n - 1)],
            send_sem=send_sem.at[0], recv_sem=recv_sem.at[0],
            device_id=(lax.rem(me + 1, n), tn), device_id_type=MESH,
        )

    for j in range(1, n):
        exchange(oq, aq, q_send, q_recv, j).start()
    pump(1)

    loads[1].wait()
    own_keys = dot(normed, w_ref[1]).astype(BF16)
    loads[2].wait()
    own_values = dot(normed, w_ref[2]).astype(BF16)

    loads[3].wait()
    piece = min(128, span)
    braw_rows = braw.reshape(2 * span, width)

    branch_pick = splitter(piece)

    def part_branch(b, carry):
        raw = braw_rows[pl.ds(pl.multiple_of(2 * piece * b, 2 * piece), 2 * piece), :]
        k_part, v_part = split_rows(branch_pick, raw)
        at = pl.ds(pl.multiple_of(piece * b, piece), piece)
        kbr[at, :] = k_part
        vbr[at, :] = v_part
        return carry

    lax.fori_loop(0, span // piece, part_branch, 0, unroll=2)

    col_head = div(iota((1, gw), 1), HD)

    def stack(part):
        return jnp.concatenate(
            [jnp.where(col_head == h, part, 0.0) for h in range(hg)], axis=0
        ).astype(BF16)

    def attend(scores, mask, values):
        peaks, sums, weights = [], [], []
        for s, keep in zip(scores, mask):
            if keep is not None:
                s = jnp.where(keep, s, -1e30)
            peak = jnp.max(s, axis=1, keepdims=True)
            w = jnp.exp2((s - peak) * SCALE)
            peaks.append(peak)
            sums.append(jnp.sum(w, axis=1, keepdims=True))
            weights.append(w.astype(BF16))
        weighted = dot(jnp.concatenate(weights, axis=0), values)
        return peaks, sums, weighted

    def attend_long(stacked_rows, keys_of, values_of, keep, step):
        amount_of, length = stacked_rows.shape[0], keys_of.shape[0]
        sbuf[:amount_of, :length] = dot_t(stacked_rows, keys_of)

        def some(c, carry):
            for part in range(0, step, 32):
                at = pl.ds(pl.multiple_of(c * step + part, 32), 32)
                s = sbuf[at, :length]
                if keep is not None:
                    s = jnp.where(keep, s, -1e30)
                peak = jnp.max(s, axis=1, keepdims=True)
                w = jnp.exp2((s - peak) * SCALE)
                peak_buf[at, :] = jnp.broadcast_to(peak, (32, 128))
                sum_buf[at, :] = jnp.broadcast_to(jnp.sum(w, axis=1, keepdims=True), (32, 128))
                pbuf[at, :length] = w.astype(BF16)
            return carry

        lax.fori_loop(0, amount_of // step, some, 0)
        weighted = dot(pbuf[:amount_of, :length], values_of)
        return peak_buf[:amount_of, :1], sum_buf[:amount_of, :1], weighted

    loads[4].wait()
    leaf_rows = requests * leaf_span
    lpiece = min(128, leaf_rows)
    lraw_rows = lraw.reshape(2 * leaf_rows, width)

    leaf_pick = branch_pick if lpiece == piece else splitter(lpiece)

    def part_leaf(b, carry):
        raw = lraw_rows[pl.ds(pl.multiple_of(2 * lpiece * b, 2 * lpiece), 2 * lpiece), :]
        k_part, v_part = split_rows(leaf_pick, raw)
        at = pl.ds(pl.multiple_of(lpiece * b, lpiece), lpiece)
        kloc[at, :] = k_part
        vloc[at, :] = v_part
        return carry

    lax.fori_loop(0, leaf_rows // lpiece, part_leaf, 0, unroll=2)
    kloc[pl.ds(leaf_rows, rows), :] = own_keys
    vloc[pl.ds(leaf_rows, rows), :] = own_values
    keys = leaf_rows + rows
    leaf_len = per_row(llen_ref[...])
    new_count = per_row(newc_ref[...])
    ki, kj = iota((rows, keys), 0), iota((rows, keys), 1)
    own_j = kj - leaf_rows
    draft_j = rem(jnp.maximum(own_j, 0), drafts)
    in_leaf = (
        (div(kj, leaf_span) == div(ki, drafts))
        & (rem(kj, leaf_span).astype(F32) < leaf_len)
    )
    in_own = (
        (div(jnp.maximum(own_j, 0), drafts) == div(ki, drafts))
        & (draft_j <= rem(ki, drafts))
        & (draft_j.astype(F32) < new_count)
    )
    local_keep = ((kj < leaf_rows) & in_leaf) | ((kj >= leaf_rows) & in_own)
    stacked = [stack(queries[:, g * gw : (g + 1) * gw].astype(F32)) for g in range(groups)]
    local_states = []
    for g in range(groups):
        cols = slice(g * gw, (g + 1) * gw)
        scores = dot_t(stacked[g], kloc[:, cols])
        pieces = [scores[h * rows : (h + 1) * rows] for h in range(hg)]
        local_states.append(attend(pieces, [local_keep] * hg, vloc[:, cols]))

    if half >= 2:
        pump(2)

    of_all(oq, aq, q_send, q_recv).wait_recv()
    asked[...] = aq[...].astype(F32)
    owned = jnp.sum(
        jnp.where(owner_ref[...] == me, blen_ref[...], 0).astype(F32), axis=1, keepdims=True
    )
    usable = iota((1, span), 1).astype(F32) < owned
    count = n * cd
    lane = iota((1, 128), 1)
    slabs = []
    for g in range(groups):
        part = asked[:, g * cd : (g + 1) * cd, :].reshape(count, gw)
        cols = slice(g * gw, (g + 1) * gw)
        peaks, sums, weighted = attend_long(stack(part), kbr[:, cols], vbr[:, cols], usable, 256)
        inverse = 1.0 / sums
        level = peaks * SCALE + jnp.log(sums) * LOG2E
        mixed = jnp.zeros((count, gw), F32)
        levels = jnp.zeros((count, 128), F32)
        for h in range(hg):
            at = slice(h * count, (h + 1) * count)
            mixed = jnp.where(col_head == h, weighted[at] * inverse[at], mixed)
            levels = jnp.where(rem(lane, hg) == h, level[at], levels)
        high = levels.astype(BF16).astype(F32)
        middle = (levels - high).astype(BF16).astype(F32)
        low = levels - high - middle
        stats = jnp.where(lane < hg, high, jnp.where(lane < 2 * hg, middle, low))
        stats = jnp.where(lane < 3 * hg, stats, 0.0)
        slabs.append(jnp.concatenate([mixed, stats], axis=1).reshape(n, cd, gw + 128))
        if half >= 3 and g == 0:
            pump(3)
    if groups * cd < slot:
        slabs.append(jnp.zeros((n, slot - groups * cd, gw + 128), F32))
    bo[...] = jnp.concatenate(slabs, axis=1).astype(BF16)
    br[me] = bo[me]
    for j in range(1, n):
        exchange(bo, br, b_send, b_recv, j).start()

    for hop in range(4, half + 1):
        pump(hop)
    for index, offset in shared:
        share(index, offset, False).wait_recv()

    before = []
    for g in range(groups):
        cols = slice(g * gw, (g + 1) * gw)
        root_keys = kvroot[:, 0, :, cols].reshape(n * block, gw)
        root_values = kvroot[:, 1, :, cols].reshape(n * block, gw)
        peaks, sums, weighted = attend_long(stacked[g], root_keys, root_values, None, min(256, hg * rows))
        lpeaks, lsums, lweighted = local_states[g]
        level = jnp.zeros((rows, gw), F32)
        amount = jnp.zeros((rows, gw), F32)
        mixed = jnp.zeros((rows, gw), F32)
        for h in range(hg):
            at = slice(h * rows, (h + 1) * rows)
            top = jnp.maximum(peaks[at], lpeaks[h])
            one = jnp.exp2((peaks[at] - top) * SCALE)
            two = jnp.exp2((lpeaks[h] - top) * SCALE)
            level = jnp.where(col_head == h, top * SCALE, level)
            amount = jnp.where(col_head == h, one * sums[at] + two * lsums[h], amount)
            mixed = jnp.where(col_head == h, one * weighted[at] + two * lweighted[at], mixed)
        before.append((level, amount, mixed))

    group_l, item_l, draft_l = slot_parts((rows, total), 1)
    take = (dot_t(target, spread) > 0.5) & (order_col == item_l) & (
        rem(iota((rows, total), 0), drafts) == draft_l
    )
    takes = [jnp.where(take & (group_l == g), 1.0, 0.0).astype(BF16) for g in range(groups)]
    loads[5].wait()

    of_all(bo, br, b_send, b_recv).wait_recv()
    flat = br[...].reshape(total, gw + 128)
    heads = []
    for g in range(groups):
        got = dot(takes[g], flat)
        stats = got[:, gw:]
        level, amount, mixed = before[g]
        other = jnp.zeros((rows, gw), F32)
        for h in range(hg):
            joined = (
                stats[:, h : h + 1]
                + stats[:, hg + h : hg + h + 1]
                + stats[:, 2 * hg + h : 2 * hg + h + 1]
            )
            other = jnp.where(col_head == h, joined, other)
        top = jnp.maximum(level, other)
        one = jnp.exp2(level - top)
        two = jnp.exp2(other - top)
        heads.append(((one * mixed + two * got[:, :gw]) / (one * amount + two)).astype(BF16))
    attention = heads[0] if groups == 1 else jnp.concatenate(heads, axis=1)
    ow = out_ref.shape[1]

    def reduce_copy(j, outgoing):
        there = lax.rem(tn + j, nt)
        here = tn if outgoing else lax.rem(tn + nt - j, nt)
        return pltpu.make_async_remote_copy(
            src_ref=tb.at[there], dst_ref=tr.at[here],
            send_sem=t_send.at[j], recv_sem=t_recv.at[j],
            device_id=(me, there), device_id_type=MESH,
        )

    def term(t):
        return dot(attention, wout_ref[:, pl.ds(pl.multiple_of(t * ow, ow), ow)])

    for j in range(1, nt):
        there = lax.rem(tn + j, nt)
        tb[there] = term(there).astype(BF16)
        reduce_copy(j, True).start()
    in_use = rem(iota((rows, 1), 0), drafts).astype(F32) < new_count
    result = term(tn)
    of_all(kvroot, kvroot, root_send, root_send).wait_send()
    of_all(oq, aq, q_send, q_recv).wait_send()
    of_all(bo, br, b_send, b_recv).wait_send()
    for j in range(1, nt):
        reduce_copy(j, False).wait_recv()
        result = result + tr[lax.rem(tn + nt - j, nt)].astype(F32)
    out_ref[...] = jnp.where(in_use, result, 0.0).astype(BF16)
    for j in range(1, nt):
        reduce_copy(j, True).wait_send()


def local(
    n, nt,
    tokens, norm_gain, w_qkv, w_out, root_kv, branch_kv, leaf_kv,
    branch, node_owner, branch_len, leaf_len, new_count,
):
    rows, depth = tokens.shape
    requests = branch.shape[0]
    drafts = rows // requests
    nodes = node_owner.shape[0]
    width = w_out.shape[0]
    ow = w_out.shape[1] // nt
    cap = max(2, 2 * requests // nodes)
    gw = min(width, 256)
    slot = max(16, width // gw * cap * drafts)
    block = root_kv.shape[0]
    span = branch_kv.shape[1]
    leaf_rows = leaf_kv.shape[0] * leaf_kv.shape[1]
    half = n // 4
    long_rows = gw // HD * max(n * cap * drafts, rows)
    longest = max(span, n * block)
    vmem = pl.BlockSpec(memory_space=pltpu.VMEM)
    hbm = pl.BlockSpec(memory_space=pl.ANY)
    dma = pltpu.SemaphoreType.DMA
    return pl.pallas_call(
        functools.partial(kernel, n, nt, drafts, cap),
        out_shape=jax.ShapeDtypeStruct((rows, ow), BF16),
        in_specs=[vmem, vmem, hbm, hbm, vmem, hbm, hbm] + [vmem] * 5,
        out_specs=vmem,
        scratch_shapes=[
            pltpu.VMEM((3, depth, width), BF16),
            pltpu.VMEM(w_out.shape, BF16),
            pltpu.VMEM((span, 2, width), BF16),
            pltpu.VMEM((leaf_rows, 2, width), BF16),
            pltpu.VMEM((n, 2, block, width), BF16),
            pltpu.VMEM((span, width), BF16),
            pltpu.VMEM((span, width), BF16),
            pltpu.VMEM((leaf_rows + rows, width), BF16),
            pltpu.VMEM((leaf_rows + rows, width), BF16),
            pltpu.VMEM((n, slot, gw), BF16),
            pltpu.VMEM((n, slot, gw), BF16),
            pltpu.VMEM((n, slot, gw + 128), BF16),
            pltpu.VMEM((n, slot, gw + 128), BF16),
            pltpu.VMEM((nt, rows, ow), BF16),
            pltpu.VMEM((nt, rows, ow), BF16),
            pltpu.VMEM((long_rows, longest), F32),
            pltpu.VMEM((long_rows, longest), BF16),
            pltpu.VMEM((long_rows, 128), F32),
            pltpu.VMEM((long_rows, 128), F32),
            pltpu.VMEM((n, slot, gw), F32),
            dma((6,)),
            dma((1,)),
            dma((2, half + 1)),
            dma((2 * half,)),
            dma((1,)),
            dma((1,)),
            dma((1,)),
            dma((1,)),
            dma((nt,)),
            dma((nt,)),
        ],
        compiler_params=pltpu.CompilerParams(
            collective_id=0, has_side_effects=True, vmem_limit_bytes=58 << 20
        ),
    )(
        tokens,
        norm_gain.reshape(1, -1),
        jnp.transpose(w_qkv, (1, 0, 2)),
        w_out,
        root_kv,
        branch_kv.reshape(span, 2, width),
        leaf_kv.reshape(leaf_rows, 2, width),
        branch.reshape(1, requests),
        node_owner.reshape(1, nodes),
        branch_len.reshape(1, nodes),
        leaf_len.reshape(1, requests),
        new_count.reshape(1, requests),
    )


def solution(mesh):
    placed = (
        P("req", None),
        P(),
        P(None, None, "tensor"),
        P("tensor", None),
        P("req", None, "tensor"),
        P("req", None, None, "tensor"),
        P("req", None, None, "tensor"),
        P("req", None),
        P(),
        P(),
        P("req"),
        P("req"),
    )
    return jax.shard_map(
        functools.partial(local, mesh.shape["req"], mesh.shape["tensor"]),
        mesh=mesh, in_specs=placed, out_specs=P("req", "tensor"), check_vma=False,
    )
```
